128 devices in a mesh: row: 8 (over z, core), col: 8 (over x, y_hi), layer: 2 (over y_lo).
Axes of the slice: x: 4, y: 4 (y_hi: 2, y_lo: 2; y = y_hi * 2 + y_lo), z: 4, core: 2. Of those that a mesh axis runs over, the one named last changes fastest.
Arguments:
- stored_blocks: float32 [8, 8, 48, 128, 128], P('row', 'col'), as said below
- pattern: int32 [8, 8, 48], replicated, may hold values from -1 to 47, as said below
- result_cols: int32 [8, 8, 48, 2], P('row', 'col'), may hold values from 0 to 47, as said below
Outputs:
- result_blocks: float32 [8, 8, 48, 2, 128, 128], P('row', 'col', 'layer')
The draws below stay inside these ranges and needn't reach their ends.
Inputs may be any that keep to these rules, and one draw needn't show every extreme that they name: Each block row of a tile holds at most one block. The pattern is symmetric: pattern(i, j, r) = c exactly when pattern(j, i, c) = r. Diagonal tiles hold just the diagonal blocks: pattern(i, i, r) = r. `result_cols`: the 2 columns listed for one block row of a tile are distinct. X is symmetric. stored_blocks(i, j, r) holds the block at local row r and local column pattern(i, j, r) of tile (i, j) when that block is upper; every other slot is zero.
All inputs are finite; a program needn't handle non-finite values.
Results may differ from the reference program's by a relative error of at most 0.0003.
Values sent between devices are 32-bit elements; how exact they have to be, the bound alone decides.
A program may use at most 128 MiB of HBM per device.

```python
import jax
import jax.numpy as jnp
from jax import lax

BS = 128
KR = 2
GRID = 8
BR = 48


def permute_rows(row_key):
    return jax.random.permutation(row_key, BR)


def block_pattern(key):
    pair_keys = jax.random.split(jax.random.fold_in(key, 17), GRID * GRID)
    orders = jax.vmap(permute_rows)(pair_keys).reshape(GRID, GRID, BR).astype(jnp.int32)
    inverse = jnp.argsort(orders, axis=-1).astype(jnp.int32)
    tile_row = jnp.arange(GRID)[:, None, None]
    tile_col = jnp.arange(GRID)[None, :, None]
    spacing = jnp.abs(tile_row - tile_col)
    distance = jnp.minimum(spacing, GRID - spacing)
    chance = jax.random.randint(jax.random.fold_in(key, 23), (GRID, GRID, BR), 0, 2 * GRID)
    kept = chance >= 2 * distance - 1
    inverse_swapped = jnp.swapaxes(inverse, 0, 1)
    kept_mirror = jnp.take_along_axis(jnp.swapaxes(kept, 0, 1), inverse_swapped, axis=-1)
    local_rows = jnp.broadcast_to(jnp.arange(BR, dtype=jnp.int32)[None, None, :], (GRID, GRID, BR))
    upper_cols = jnp.where(kept, orders, -1)
    lower_cols = jnp.where(kept_mirror, inverse_swapped, -1)
    chosen = jnp.where(tile_row == tile_col, local_rows, jnp.where(tile_row < tile_col, upper_cols, lower_cols))
    return chosen.astype(jnp.int32)


def draw_pattern(key, part):
    return block_pattern(key)


def draw_result_cols(key, part):
    pattern = block_pattern(key)
    tile_row = jnp.arange(GRID)[:, None, None]
    tile_col = jnp.arange(GRID)[None, :, None]
    local_rows = jnp.arange(BR)[None, None, :]
    spare_first = jax.random.randint(jax.random.fold_in(key, 31), (GRID, GRID, BR), 0, BR)
    first = jnp.where(pattern >= 0, pattern, spare_first)
    middle = jax.random.randint(jax.random.fold_in(key, 37), (GRID, GRID, BR), 0, GRID)
    step_cols = pattern[tile_row, middle, local_rows]
    reach = pattern[middle, tile_col, jnp.maximum(step_cols, 0)]
    valid = (step_cols >= 0) & (reach >= 0) & (reach != first)
    spare_second = (first + 1 + jax.random.randint(jax.random.fold_in(key, 41), (GRID, GRID, BR), 0, BR - 1)) % BR
    second = jnp.where(valid, reach, spare_second)
    return jnp.stack([first, second], axis=-1).astype(jnp.int32)


def draw_stored_blocks(key, part):
    pattern = block_pattern(key)
    safe_cols = jnp.maximum(pattern, 0)
    scale = BS ** (-0.25)
    raw = jax.random.normal(jax.random.fold_in(key, 53), (GRID, GRID, BR, BS, BS), jnp.float32) * scale
    gains = jnp.exp(0.1 * jax.random.normal(jax.random.fold_in(key, 59), (GRID, BR), jnp.float32))
    tile_row = jnp.arange(GRID)[:, None, None]
    tile_col = jnp.arange(GRID)[None, :, None]
    local_rows = jnp.arange(BR)[None, None, :]
    mirrored = jnp.swapaxes(jnp.swapaxes(raw, 0, 1)[tile_row, tile_col, safe_cols], -1, -2)
    symmetric = (raw + jnp.swapaxes(raw, -1, -2)) * 0.5 ** 0.5
    values = jnp.where((tile_row == tile_col)[..., None, None], symmetric, jnp.where((tile_row < tile_col)[..., None, None], raw, mirrored))
    row_gain = gains[tile_row, local_rows]
    col_gain = gains[jnp.broadcast_to(tile_col, (GRID, GRID, BR)), safe_cols]
    values = values * (row_gain * col_gain)[..., None, None]
    stored = (pattern >= 0) & (local_rows * GRID + tile_row <= safe_cols * GRID + tile_col)
    return jnp.where(stored[..., None, None], values, 0.0).astype(jnp.float32)


def setup_inputs(seed: int = 0) -> dict:
    streams_of = jax.random.split(jax.random.key(seed), 4)
    stored_blocks = draw_stored_blocks(jax.random.fold_in(streams_of[3], 71), 0)
    pattern = draw_pattern(jax.random.fold_in(streams_of[3], 71), 0)
    result_cols = draw_result_cols(jax.random.fold_in(streams_of[3], 71), 0)
    return {"stored_blocks": stored_blocks, "pattern": pattern, "result_cols": result_cols}


def complete_tiles(stored_blocks, pattern):
    tile_row = jnp.arange(GRID)[:, None, None]
    tile_col = jnp.arange(GRID)[None, :, None]
    local_rows = jnp.arange(BR)[None, None, :]
    safe_cols = jnp.maximum(pattern, 0)
    is_upper = local_rows * GRID + tile_row <= safe_cols * GRID + tile_col
    mirrored = jnp.swapaxes(jnp.swapaxes(stored_blocks, 0, 1)[tile_row, tile_col, safe_cols], -1, -2)
    return jnp.where(is_upper[..., None, None], stored_blocks, mirrored)


def accumulate(totals, left_tile, right_tile, left_cols, right_cols, wanted):
    inner_rows = jnp.maximum(left_cols, 0)
    partner = right_tile[inner_rows]
    target = right_cols[inner_rows]
    present = (left_cols >= 0) & (target >= 0)
    products = jnp.einsum("rab,rbc->rac", left_tile.astype(jnp.float32), partner.astype(jnp.float32), precision=lax.Precision.HIGHEST)
    matched = (present[:, None] & (wanted == target[:, None])).astype(jnp.float32)
    return totals + matched[:, :, None, None] * products[:, None]


def reference(stored_blocks, pattern, result_cols):
    full_tiles = complete_tiles(stored_blocks, pattern)

    def tile_product(flat):
        tile_row = flat // GRID
        tile_col = flat % GRID
        totals = jnp.zeros((BR, KR, BS, BS), jnp.float32)
        for middle in range(GRID):
            totals = accumulate(totals, full_tiles[tile_row, middle], full_tiles[middle, tile_col], pattern[tile_row, middle], pattern[middle, tile_col], result_cols[tile_row, tile_col])
        return totals

    summed = lax.map(tile_product, jnp.arange(GRID * GRID))
    return summed.reshape(GRID, GRID, BR, KR, BS, BS)
```

```python
import functools

import jax
import jax.numpy as jnp
from jax import lax
from jax.experimental import pallas as pl
from jax.experimental.pallas import tpu as pltpu
from jax.sharding import PartitionSpec as P

MESH = pl.DeviceIdType.MESH
CHUNKS = 3


def product(a, b):
    a_hi = a.astype(jnp.bfloat16)
    a_lo = (a - a_hi.astype(jnp.float32)).astype(jnp.bfloat16)
    b_hi = b.astype(jnp.bfloat16)
    b_lo = (b - b_hi.astype(jnp.float32)).astype(jnp.bfloat16)
    left = jnp.concatenate([a_hi, a_lo, a_hi], axis=1)
    right = jnp.concatenate([b_hi, b_hi, b_lo], axis=0)
    return jnp.dot(left, right, preferred_element_type=jnp.float32)


def kernel(
    rows,
    pattern,
    wanted,
    stored,
    out,
    mirror_out,
    mirror_in,
    left,
    same0,
    same1,
    same2,
    same3,
    other0,
    other1,
    other2,
    other3,
    mirror_s,
    mirror_r,
    layer_s,
    layer_r,
    y_s,
    y_r,
    x_s,
    x_r,
    xf_s,
    xf_r,
    z_s,
    z_r,
    zf_s,
    zf_r,
    core_s,
    core_r,
):
    half = rows // 2
    step = half // CHUNKS
    row = lax.axis_index("row")
    col = lax.axis_index("col")
    lay = lax.axis_index("layer")
    z, k = row // 2, row % 2
    x, yh = col // 2, col % 2
    same = [same0, same1, same2, same3]
    other = [other0, other1, other2, other3]
    off_diagonal = row != col

    to_layer = {"layer": 1 - lay}
    to_y = {"col": 2 * x + (1 - yh)}
    to_core = {"row": 2 * z + (1 - k)}
    to_x = [{"col": (col + 2) % 8}, {"col": (col + 6) % 8}]
    to_z = [{"row": (row + 2) % 8}, {"row": (row + 6) % 8}]
    to_mirror = {"row": col, "col": row}

    barrier = pltpu.get_barrier_semaphore()
    for device in [to_layer, to_y, to_core, *to_x, *to_z]:
        pl.semaphore_signal(barrier, inc=1, device_id=device, device_id_type=MESH)

    @pl.when(off_diagonal)
    def _():
        pl.semaphore_signal(barrier, inc=1, device_id=to_mirror, device_id_type=MESH)

    def copy(source, target, send, recv, device):
        return pltpu.make_async_remote_copy(
            src_ref=source,
            dst_ref=target,
            send_sem=send,
            recv_sem=recv,
            device_id=device,
            device_id_type=MESH,
        )

    def part(h, ch):
        return pl.ds(h * half + ch * step, step)

    def piece(ch):
        return pl.ds(ch * step, step)

    def half_of(differs):
        return lay if differs == 0 else 1 - lay

    def mirror_copy(ch):
        return copy(mirror_out.at[piece(ch)], mirror_in.at[piece(ch)], mirror_s.at[ch], mirror_r.at[ch], to_mirror)

    def layer_copy(ch):
        at = part(lay, ch)
        return copy(same0.at[at], same0.at[at], layer_s.at[ch], layer_r.at[ch], to_layer)

    def y_copy(ch):
        return copy(left.at[0, piece(ch)], left.at[1, piece(ch)], y_s.at[ch], y_r.at[ch], to_y)

    def x_copy(way, s, ch):
        slot = (6 if way == 0 else 2) + s
        return copy(left.at[s, piece(ch)], left.at[slot, piece(ch)], x_s.at[way, s, ch], x_r.at[way, s, ch], to_x[way])

    def x_forward(way, ch):
        slot = 6 if way == 0 else 3
        return copy(left.at[slot, piece(ch)], left.at[4 + way, piece(ch)], xf_s.at[way, ch], xf_r.at[way, ch], to_x[way])

    def z_copy(way, d, ch):
        at = part(half_of(d), ch)
        target = same3 if way == 0 else same1
        return copy(same0.at[at], target.at[at], z_s.at[way, d, ch], z_r.at[way, d, ch], to_z[way])

    def z_forward(way, ch):
        at = part(half_of(way), ch)
        source = same3 if way == 0 else same1
        return copy(source.at[at], same2.at[at], zf_s.at[way, ch], zf_r.at[way, ch], to_z[way])

    def core_copy(dz, d, ch):
        at = part(half_of(d), ch)
        return copy(same[dz].at[at], other[dz].at[at], core_s.at[dz, d, ch], core_r.at[dz, d, ch], to_core)

    def each(body):
        def run(ch, carry):
            body(ch)
            return carry

        lax.fori_loop(0, CHUNKS, run, 0)

    pl.semaphore_wait(barrier, jnp.where(off_diagonal, 8, 7))

    @pl.when(off_diagonal)
    def _():
        def send_mirrored(ch):
            def pick(n, carry):
                at = ch * step + n
                source = pattern[(col * 8 + row) * rows + lay * half + at]
                mirror_out[at] = stored[jnp.maximum(source, 0)].T
                return carry

            lax.fori_loop(0, step, pick, 0)
            mirror_copy(ch).start()

        each(send_mirrored)

    def clear(n, carry):
        out[n] = jnp.zeros(out.shape[1:], out.dtype)
        return carry

    lax.fori_loop(0, half, clear, 0)

    def complete(ch):
        @pl.when(off_diagonal)
        def _():
            mirror_copy(ch).wait_recv()

            def choose(n, carry):
                at = ch * step + n
                r = lay * half + at
                c = jnp.maximum(pattern[(row * 8 + col) * rows + r], 0)
                upper = r * 8 + row <= c * 8 + col
                block = jnp.where(upper, stored[r], mirror_in[at])
                same0[r] = block
                left[0, at] = block
                return carry

            lax.fori_loop(0, step, choose, 0)

        @pl.when(jnp.logical_not(off_diagonal))
        def _():
            def take(n, carry):
                at = ch * step + n
                block = stored[lay * half + at]
                same0[lay * half + at] = block
                left[0, at] = block
                return carry

            lax.fori_loop(0, step, take, 0)

        layer_copy(ch).start()
        y_copy(ch).start()
        for way in range(2):
            x_copy(way, 0, ch).start()
            z_copy(way, 0, ch).start()
        core_copy(0, 0, ch).start()

    each(complete)

    def spread(ch):
        layer_copy(ch).wait_recv()
        for way in range(2):
            z_copy(way, 1, ch).start()
        core_copy(0, 1, ch).start()
        y_copy(ch).wait_recv()
        for way in range(2):
            x_copy(way, 1, ch).start()

    each(spread)

    def forward_first(ch):
        x_copy(0, 0, ch).wait_recv()
        x_forward(0, ch).start()
        z_copy(0, 0, ch).wait_recv()
        z_forward(0, ch).start()
        core_copy(3, 0, ch).start()
        z_copy(1, 0, ch).wait_recv()
        core_copy(1, 0, ch).start()

    each(forward_first)

    def forward_second(ch):
        x_copy(1, 1, ch).wait_recv()
        x_forward(1, ch).start()
        z_copy(1, 1, ch).wait_recv()
        z_forward(1, ch).start()
        core_copy(1, 1, ch).start()
        z_copy(0, 1, ch).wait_recv()
        core_copy(3, 1, ch).start()

    each(forward_second)

    def near(ch):
        x_copy(1, 0, ch).wait_recv()
        x_copy(0, 1, ch).wait_recv()
        for dz in (0, 1, 3):
            for d in range(2):
                core_copy(dz, d, ch).wait_recv()

    each(near)

    def multiply(dz, differs):
        tile = (other if differs else same)[dz]
        m = 2 * ((z + dz) % 4) + (k + differs) % 2
        slot = 2 * ((m // 2 + 4 - x) % 4) + (m % 2 + yh) % 2

        def one(n, carry):
            r = lay * half + n
            c = pattern[(row * 8 + m) * rows + r]
            inner = jnp.maximum(c, 0)
            t = pattern[(m * 8 + col) * rows + inner]
            present = jnp.logical_and(c >= 0, t >= 0)
            block = product(left[slot, n], tile[inner])
            for q in range(2):
                matched = jnp.logical_and(present, wanted[2 * r + q] == t)
                out[n, q] += block * jnp.where(matched, 1.0, 0.0)
            return carry

        lax.fori_loop(0, half, one, 0, unroll=4)

    def far(dz):
        return (z + dz - x + 4) % 4 == 2

    for dz in (0, 1, 3):
        @pl.when(jnp.logical_not(far(dz)))
        def _(dz=dz):
            multiply(dz, 0)
            multiply(dz, 1)

    def last(ch):
        for way in range(2):
            z_forward(way, ch).wait_recv()
            core_copy(2, way, ch).start()
            x_forward(way, ch).wait_recv()

    each(last)

    for dz in (0, 1, 3):
        @pl.when(far(dz))
        def _(dz=dz):
            multiply(dz, 0)
            multiply(dz, 1)

    multiply(2, 0)

    def last_core(ch):
        for d in range(2):
            core_copy(2, d, ch).wait_recv()

    each(last_core)
    multiply(2, 1)

    def drain(ch):
        @pl.when(off_diagonal)
        def _():
            mirror_copy(ch).wait_send()

        layer_copy(ch).wait_send()
        y_copy(ch).wait_send()
        for way in range(2):
            x_forward(way, ch).wait_send()
            z_forward(way, ch).wait_send()
            for d in range(2):
                x_copy(way, d, ch).wait_send()
                z_copy(way, d, ch).wait_send()
        for dz in range(4):
            for d in range(2):
                core_copy(dz, d, ch).wait_send()

    each(drain)


def per_device(stored_blocks, pattern, result_cols):
    tile = stored_blocks[0, 0]
    rows, size = tile.shape[0], tile.shape[-1]
    half = rows // 2
    vmem = pl.BlockSpec(memory_space=pltpu.VMEM)
    smem = pl.BlockSpec(memory_space=pltpu.SMEM)
    sems = pltpu.SemaphoreType.DMA
    block = (size, size)
    result = pl.pallas_call(
        functools.partial(kernel, rows),
        out_shape=jax.ShapeDtypeStruct((half, 2, *block), jnp.float32),
        in_specs=[smem, smem, vmem],
        out_specs=vmem,
        scratch_shapes=[
            pltpu.VMEM((half, *block), jnp.float32),
            pltpu.VMEM((half, *block), jnp.float32),
            pltpu.VMEM((8, half, *block), jnp.float32),
            *[pltpu.VMEM((rows, *block), jnp.float32)] * 8,
            *[sems((CHUNKS,))] * 6,
            *[sems((2, 2, CHUNKS))] * 2,
            *[sems((2, CHUNKS))] * 2,
            *[sems((2, 2, CHUNKS))] * 2,
            *[sems((2, CHUNKS))] * 2,
            *[sems((4, 2, CHUNKS))] * 2,
        ],
        compiler_params=pltpu.CompilerParams(
            collective_id=0, has_side_effects=True, vmem_limit_bytes=58 * 2**20
        ),
    )(pattern.reshape(-1), result_cols.reshape(-1), tile)
    return result[None, None]


def solution(mesh):
    return jax.shard_map(
        per_device,
        mesh=mesh,
        in_specs=(P("row", "col", None, None, None), P(), P("row", "col", None, None)),
        out_specs=P("row", "col", "layer", None, None, None),
        check_vma=False,
    )
```

```python
import functools

import jax
import jax.numpy as jnp
from jax import lax
from jax.experimental import pallas as pl
from jax.experimental.pallas import tpu as pltpu
from jax.sharding import PartitionSpec as P

MESH = pl.DeviceIdType.MESH
CHUNKS = 3


def product(a, b):
    a_hi = a.astype(jnp.bfloat16)
    a_lo = (a - a_hi.astype(jnp.float32)).astype(jnp.bfloat16)
    b_hi = b.astype(jnp.bfloat16)
    b_lo = (b - b_hi.astype(jnp.float32)).astype(jnp.bfloat16)
    left = jnp.concatenate([a_hi, a_lo, a_hi], axis=1)
    right = jnp.concatenate([b_hi, b_hi, b_lo], axis=0)
    return jnp.dot(left, right, preferred_element_type=jnp.float32)


def kernel(
    rows,
    pattern,
    wanted,
    stored,
    out,
    mirror_out,
    mirror_in,
    swapped,
    passing,
    left,
    same0,
    same1,
    same2,
    same3,
    other0,
    other1,
    other2,
    other3,
    mirror_s,
    mirror_r,
    swap_s,
    swap_r,
    pass_s,
    pass_r,
    layer_s,
    layer_r,
    y_s,
    y_r,
    x_s,
    x_r,
    xf_s,
    xf_r,
    z_s,
    z_r,
    zf_s,
    zf_r,
    core_s,
    core_r,
):
    half = rows // 2
    step = half // CHUNKS
    sub = step // 2
    row = lax.axis_index("row")
    col = lax.axis_index("col")
    lay = lax.axis_index("layer")
    z, k = row // 2, row % 2
    x, yh = col // 2, col % 2
    same = [same0, same1, same2, same3]
    other = [other0, other1, other2, other3]
    on_ring = x == z
    crossed = k != yh
    off_diagonal = jnp.logical_or(jnp.logical_not(on_ring), crossed)

    to_layer = {"layer": 1 - lay}
    to_y = {"col": 2 * x + (1 - yh), "layer": 1 - lay}
    to_core = {"row": 2 * z + (1 - k)}
    to_x = [{"col": (col + 2) % 8}, {"col": (col + 6) % 8}]
    to_z = [{"row": (row + 2) % 8}, {"row": (row + 6) % 8}]
    to_straight = {"row": 2 * x + k, "col": 2 * z + yh}
    to_crossed = {"row": 2 * z + yh, "col": 2 * x + k}
    pass_out = {"row": 2 * x + yh, "col": 2 * x + k}
    pass_in = {"row": row, "col": 2 * z + yh}
    pass_from = [{"row": 2 * ((z + dz) % 4) + yh, "col": 2 * x + k} for dz in (1, 2, 3)]
    pass_on = [{"row": row, "col": 2 * ((z + dz) % 4) + yh} for dz in (1, 2, 3)]

    barrier = pltpu.get_barrier_semaphore()

    def greet(devices):
        for device in devices:
            pl.semaphore_signal(barrier, inc=1, device_id=device, device_id_type=MESH)

    greet([to_layer, to_y, to_core, *to_x, *to_z])

    @pl.when(crossed)
    def _():
        greet([to_crossed])

    @pl.when(on_ring)
    def _():
        greet(pass_from + pass_on)

    @pl.when(jnp.logical_not(on_ring))
    def _():
        greet([to_straight, pass_out, pass_in])

    def copy(source, target, send, recv, device):
        return pltpu.make_async_remote_copy(
            src_ref=source,
            dst_ref=target,
            send_sem=send,
            recv_sem=recv,
            device_id=device,
            device_id_type=MESH,
        )

    def part(h, ch):
        return pl.ds(h * half + ch * step, step)

    def piece(ch):
        return pl.ds(ch * step, step)

    def half_of(differs):
        return lay if differs == 0 else 1 - lay

    def mirror_part(p, ch):
        return pl.ds(ch * step + p * sub, sub)

    def mirror_copy(p, ch, device):
        at = mirror_part(p, ch)
        return copy(mirror_out.at[at], mirror_in.at[at], mirror_s.at[p, ch], mirror_r.at[p, ch], device)

    def swap_copy(ch):
        at = pl.ds(ch * sub, sub)
        return copy(mirror_out.at[mirror_part(0, ch)], swapped.at[at], mirror_s.at[0, ch], swap_r.at[ch], to_crossed)

    def swap_on(ch):
        at = pl.ds(ch * sub, sub)
        return copy(swapped.at[at], mirror_in.at[mirror_part(0, ch)], swap_s.at[ch], mirror_r.at[0, ch], to_straight)

    def pass_copy(ch):
        at = pl.ds(ch * sub, sub)
        slot = (z - x + 4) % 4 - 1
        return copy(
            mirror_out.at[mirror_part(1, ch)], passing.at[slot, at], mirror_s.at[1, ch], pass_r.at[slot, ch], pass_out
        )

    def passing_copy(slot, ch):
        at = pl.ds(ch * sub, sub)
        return copy(
            passing.at[slot, at], mirror_in.at[mirror_part(1, ch)], pass_s.at[slot, ch], mirror_r.at[1, ch], pass_on[slot]
        )

    def arriving(slot, ch):
        at = pl.ds(ch * sub, sub)
        return copy(
            mirror_out.at[mirror_part(1, ch)], passing.at[slot, at], mirror_s.at[1, ch], pass_r.at[slot, ch], pass_from[slot]
        )

    def layer_copy(ch):
        at = part(lay, ch)
        return copy(same0.at[at], same0.at[at], layer_s.at[ch], layer_r.at[ch], to_layer)

    def y_copy(ch):
        return copy(same0.at[part(1 - lay, ch)], left.at[1, piece(ch)], y_s.at[ch], y_r.at[ch], to_y)

    def x_copy(way, s, ch):
        slot = (6 if way == 0 else 2) + s
        return copy(left.at[s, piece(ch)], left.at[slot, piece(ch)], x_s.at[way, s, ch], x_r.at[way, s, ch], to_x[way])

    def x_forward(way, ch):
        slot = 6 if way == 0 else 3
        return copy(left.at[slot, piece(ch)], left.at[4 + way, piece(ch)], xf_s.at[way, ch], xf_r.at[way, ch], to_x[way])

    def z_copy(way, d, ch):
        at = part(half_of(d), ch)
        target = same3 if way == 0 else same1
        return copy(same0.at[at], target.at[at], z_s.at[way, d, ch], z_r.at[way, d, ch], to_z[way])

    def z_forward(way, ch):
        at = part(half_of(way), ch)
        source = same3 if way == 0 else same1
        return copy(source.at[at], same2.at[at], zf_s.at[way, ch], zf_r.at[way, ch], to_z[way])

    def core_copy(dz, d, ch):
        at = part(half_of(d), ch)
        return copy(same[dz].at[at], other[dz].at[at], core_s.at[dz, d, ch], core_r.at[dz, d, ch], to_core)

    def each(body):
        def run(ch, carry):
            body(ch)
            return carry

        lax.fori_loop(0, CHUNKS, run, 0)

    pl.semaphore_wait(barrier, 7 + jnp.where(on_ring, 6, 3) + jnp.where(crossed, 1, 0))

    def send_mirrored(ch):
        def pick(n, carry):
            at = ch * step + n
            source = pattern[col, row, lay * half + at]
            mirror_out[at] = stored[jnp.maximum(source, 0)].T
            return carry

        lax.fori_loop(0, step, pick, 0)

        @pl.when(on_ring)
        def _():
            mirror_copy(0, ch, to_crossed).start()
            mirror_copy(1, ch, to_crossed).start()

        @pl.when(jnp.logical_not(on_ring))
        def _():
            @pl.when(crossed)
            def _():
                swap_copy(ch).start()

            @pl.when(jnp.logical_not(crossed))
            def _():
                mirror_copy(0, ch, to_straight).start()

            pass_copy(ch).start()

    @pl.when(off_diagonal)
    def _():
        each(send_mirrored)

    def clear(n, carry):
        out[n] = jnp.zeros(out.shape[1:], out.dtype)
        return carry

    lax.fori_loop(0, half, clear, 0)

    def straight_on(ch):
        swap_copy(ch).wait_recv()
        swap_on(ch).start()

    @pl.when(jnp.logical_and(crossed, jnp.logical_not(on_ring)))
    def _():
        each(straight_on)

    def complete(ch):
        @pl.when(off_diagonal)
        def _():
            mirror_copy(0, ch, to_straight).wait_recv()
            mirror_copy(1, ch, to_straight).wait_recv()

            def choose(n, carry):
                at = ch * step + n
                r = lay * half + at
                c = jnp.maximum(pattern[row, col, r], 0)
                upper = r * 8 + row <= c * 8 + col
                block = jnp.where(upper, stored[r], mirror_in[at])
                same0[r] = block
                left[0, at] = block
                return carry

            lax.fori_loop(0, step, choose, 0)

        @pl.when(jnp.logical_not(off_diagonal))
        def _():
            def take(n, carry):
                at = ch * step + n
                block = stored[lay * half + at]
                same0[lay * half + at] = block
                left[0, at] = block
                return carry

            lax.fori_loop(0, step, take, 0)

        layer_copy(ch).start()
        for way in range(2):
            x_copy(way, 0, ch).start()
            z_copy(way, 0, ch).start()
        core_copy(0, 0, ch).start()

        @pl.when(on_ring)
        def _():
            for slot in range(3):
                arriving(slot, ch).wait_recv()
                passing_copy(slot, ch).start()

    each(complete)

    def spread(ch):
        layer_copy(ch).wait_recv()
        y_copy(ch).start()
        for way in range(2):
            z_copy(way, 1, ch).start()
        core_copy(0, 1, ch).start()
        y_copy(ch).wait_recv()
        for way in range(2):
            x_copy(way, 1, ch).start()

    each(spread)

    def forward_first(ch):
        x_copy(0, 0, ch).wait_recv()
        x_forward(0, ch).start()
        z_copy(0, 0, ch).wait_recv()
        z_forward(0, ch).start()
        core_copy(3, 0, ch).start()
        z_copy(1, 0, ch).wait_recv()
        core_copy(1, 0, ch).start()

    each(forward_first)

    def forward_second(ch):
        x_copy(1, 1, ch).wait_recv()
        x_forward(1, ch).start()
        z_copy(1, 1, ch).wait_recv()
        z_forward(1, ch).start()
        core_copy(1, 1, ch).start()
        z_copy(0, 1, ch).wait_recv()
        core_copy(3, 1, ch).start()

    each(forward_second)

    def near(ch):
        x_copy(1, 0, ch).wait_recv()
        x_copy(0, 1, ch).wait_recv()
        for dz in (0, 1, 3):
            for d in range(2):
                core_copy(dz, d, ch).wait_recv()

    each(near)

    def multiply(dz, differs):
        tile = (other if differs else same)[dz]
        m = 2 * ((z + dz) % 4) + (k + differs) % 2
        slot = 2 * ((m // 2 + 4 - x) % 4) + (m % 2 + yh) % 2

        def one(n, carry):
            r = lay * half + n
            c = pattern[row, m, r]
            inner = jnp.maximum(c, 0)
            t = pattern[m, col, inner]
            present = jnp.logical_and(c >= 0, t >= 0)
            block = product(left[slot, n], tile[inner])
            for q in range(2):
                matched = jnp.logical_and(present, wanted[q, r] == t)
                out[n, q] += block * jnp.where(matched, 1.0, 0.0)
            return carry

        lax.fori_loop(0, half, one, 0, unroll=4)

    def far(dz):
        return (z + dz - x + 4) % 4 == 2

    for dz in (0, 1, 3):
        @pl.when(jnp.logical_not(far(dz)))
        def _(dz=dz):
            multiply(dz, 0)
            multiply(dz, 1)

    def last(ch):
        for way in range(2):
            z_forward(way, ch).wait_recv()
            core_copy(2, way, ch).start()
            x_forward(way, ch).wait_recv()

    each(last)

    for dz in (0, 1, 3):
        @pl.when(far(dz))
        def _(dz=dz):
            multiply(dz, 0)
            multiply(dz, 1)

    multiply(2, 0)

    def last_core(ch):
        for d in range(2):
            core_copy(2, d, ch).wait_recv()

    each(last_core)
    multiply(2, 1)

    def drain(ch):
        @pl.when(off_diagonal)
        def _():
            mirror_copy(0, ch, to_straight).wait_send()
            mirror_copy(1, ch, to_straight).wait_send()

        @pl.when(jnp.logical_and(crossed, jnp.logical_not(on_ring)))
        def _():
            swap_on(ch).wait_send()

        @pl.when(on_ring)
        def _():
            for slot in range(3):
                passing_copy(slot, ch).wait_send()

        layer_copy(ch).wait_send()
        y_copy(ch).wait_send()
        for way in range(2):
            x_forward(way, ch).wait_send()
            z_forward(way, ch).wait_send()
            for d in range(2):
                x_copy(way, d, ch).wait_send()
                z_copy(way, d, ch).wait_send()
        for dz in range(4):
            for d in range(2):
                core_copy(dz, d, ch).wait_send()

    each(drain)


def per_device(stored_blocks, pattern, result_cols):
    tile = stored_blocks[0, 0]
    rows, size = tile.shape[0], tile.shape[-1]
    half = rows // 2
    vmem = pl.BlockSpec(memory_space=pltpu.VMEM)
    smem = pl.BlockSpec(memory_space=pltpu.SMEM)
    sems = pltpu.SemaphoreType.DMA
    block = (size, size)
    result = pl.pallas_call(
        functools.partial(kernel, rows),
        out_shape=jax.ShapeDtypeStruct((half, 2, *block), jnp.float32),
        in_specs=[smem, smem, vmem],
        out_specs=vmem,
        scratch_shapes=[
            pltpu.VMEM((half, *block), jnp.float32),
            pltpu.VMEM((half, *block), jnp.float32),
            pltpu.VMEM((half // 2, *block), jnp.float32),
            pltpu.VMEM((3, half // 2, *block), jnp.float32),
            pltpu.VMEM((8, half, *block), jnp.float32),
            *[pltpu.VMEM((rows, *block), jnp.float32)] * 8,
            *[sems((2, CHUNKS))] * 2,
            *[sems((CHUNKS,))] * 2,
            *[sems((3, CHUNKS))] * 2,
            *[sems((CHUNKS,))] * 4,
            *[sems((2, 2, CHUNKS))] * 2,
            *[sems((2, CHUNKS))] * 2,
            *[sems((2, 2, CHUNKS))] * 2,
            *[sems((2, CHUNKS))] * 2,
            *[sems((4, 2, CHUNKS))] * 2,
        ],
        compiler_params=pltpu.CompilerParams(
            collective_id=0, has_side_effects=True, vmem_limit_bytes=58 * 2**20
        ),
    )(pattern, result_cols[0, 0].T, tile)
    return result[None, None]


def solution(mesh):
    return jax.shard_map(
        per_device,
        mesh=mesh,
        in_specs=(P("row", "col", None, None, None), P(), P("row", "col", None, None)),
        out_specs=P("row", "col", "layer", None, None, None),
        check_vma=False,
    )
```

```python
import functools

import jax
import jax.numpy as jnp
from jax import lax
from jax.experimental import pallas as pl
from jax.experimental.pallas import tpu as pltpu
from jax.sharding import PartitionSpec as P

MESH = pl.DeviceIdType.MESH
CHUNKS = 4


def product(a, b):
    a_hi = a.astype(jnp.bfloat16)
    a_lo = (a - a_hi.astype(jnp.float32)).astype(jnp.bfloat16)
    b_hi = b.astype(jnp.bfloat16)
    b_lo = (b - b_hi.astype(jnp.float32)).astype(jnp.bfloat16)
    left = jnp.concatenate([a_hi, a_lo, a_hi], axis=1)
    right = jnp.concatenate([b_hi, b_hi, b_lo], axis=0)
    return jnp.dot(left, right, preferred_element_type=jnp.float32)


def kernel(
    rows,
    pattern,
    wanted,
    stored,
    out,
    mirror_out,
    mirror_in,
    swapped,
    passing,
    left,
    same0,
    same1,
    same2,
    same3,
    other0,
    other1,
    other2,
    other3,
    mirror_s,
    mirror_r,
    swap_s,
    swap_r,
    pass_s,
    pass_r,
    layer_s,
    layer_r,
    y_s,
    y_r,
    x_s,
    x_r,
    xf_s,
    xf_r,
    z_s,
    z_r,
    zf_s,
    zf_r,
    core_s,
    core_r,
):
    half = rows // 2
    step = half // CHUNKS
    sub = step // 2
    row = lax.axis_index("row")
    col = lax.axis_index("col")
    lay = lax.axis_index("layer")
    z, k = row // 2, row % 2
    x, yh = col // 2, col % 2
    same = [same0, same1, same2, same3]
    other = [other0, other1, other2, other3]
    on_ring = x == z
    crossed = k != yh
    off_diagonal = jnp.logical_or(jnp.logical_not(on_ring), crossed)

    to_layer = {"layer": 1 - lay}
    to_y = {"col": 2 * x + (1 - yh), "layer": 1 - lay}
    to_core = {"row": 2 * z + (1 - k)}
    to_x = [{"col": (col + 2) % 8}, {"col": (col + 6) % 8}]
    to_z = [{"row": (row + 2) % 8}, {"row": (row + 6) % 8}]
    to_straight = {"row": 2 * x + k, "col": 2 * z + yh}
    to_crossed = {"row": 2 * z + yh, "col": 2 * x + k}
    pass_out = {"row": 2 * x + yh, "col": 2 * x + k}
    pass_in = {"row": row, "col": 2 * z + yh}
    pass_from = [{"row": 2 * ((z + dz) % 4) + yh, "col": 2 * x + k} for dz in (1, 2, 3)]
    pass_on = [{"row": row, "col": 2 * ((z + dz) % 4) + yh} for dz in (1, 2, 3)]

    barrier = pltpu.get_barrier_semaphore()

    def greet(devices):
        for device in devices:
            pl.semaphore_signal(barrier, inc=1, device_id=device, device_id_type=MESH)

    greet([to_layer, to_y, to_core, *to_x, *to_z])

    @pl.when(crossed)
    def _():
        greet([to_crossed])

    @pl.when(on_ring)
    def _():
        greet(pass_from + pass_on)

    @pl.when(jnp.logical_not(on_ring))
    def _():
        greet([to_straight, pass_out, pass_in])

    def copy(source, target, send, recv, device):
        return pltpu.make_async_remote_copy(
            src_ref=source,
            dst_ref=target,
            send_sem=send,
            recv_sem=recv,
            device_id=device,
            device_id_type=MESH,
        )

    def part(h, ch):
        return pl.ds(h * half + ch * step, step)

    def piece(ch):
        return pl.ds(ch * step, step)

    def half_of(differs):
        return lay if differs == 0 else 1 - lay

    def mirror_part(p, ch):
        return pl.ds(ch * step + p * sub, sub)

    def mirror_copy(p, ch, device):
        at = mirror_part(p, ch)
        return copy(mirror_out.at[at], mirror_in.at[at], mirror_s.at[p, ch], mirror_r.at[p, ch], device)

    def swap_copy(ch):
        at = pl.ds(ch * sub, sub)
        return copy(mirror_out.at[mirror_part(0, ch)], swapped.at[at], mirror_s.at[0, ch], swap_r.at[ch], to_crossed)

    def swap_on(ch):
        at = pl.ds(ch * sub, sub)
        return copy(swapped.at[at], mirror_in.at[mirror_part(0, ch)], swap_s.at[ch], mirror_r.at[0, ch], to_straight)

    def pass_copy(ch):
        at = pl.ds(ch * sub, sub)
        slot = (z - x + 4) % 4 - 1
        return copy(
            mirror_out.at[mirror_part(1, ch)], passing.at[slot, at], mirror_s.at[1, ch], pass_r.at[slot, ch], pass_out
        )

    def passing_copy(slot, ch):
        at = pl.ds(ch * sub, sub)
        return copy(
            passing.at[slot, at], mirror_in.at[mirror_part(1, ch)], pass_s.at[slot, ch], mirror_r.at[1, ch], pass_on[slot]
        )

    def arriving(slot, ch):
        at = pl.ds(ch * sub, sub)
        return copy(
            mirror_out.at[mirror_part(1, ch)], passing.at[slot, at], mirror_s.at[1, ch], pass_r.at[slot, ch], pass_from[slot]
        )

    def layer_copy(ch):
        at = part(lay, ch)
        return copy(same0.at[at], same0.at[at], layer_s.at[ch], layer_r.at[ch], to_layer)

    def y_copy(ch):
        return copy(same0.at[part(1 - lay, ch)], left.at[1, piece(ch)], y_s.at[ch], y_r.at[ch], to_y)

    def x_copy(way, s, ch):
        slot = (6 if way == 0 else 2) + s
        return copy(left.at[s, piece(ch)], left.at[slot, piece(ch)], x_s.at[way, s, ch], x_r.at[way, s, ch], to_x[way])

    def x_forward(way, ch):
        slot = 6 if way == 0 else 3
        return copy(left.at[slot, piece(ch)], left.at[4 + way, piece(ch)], xf_s.at[way, ch], xf_r.at[way, ch], to_x[way])

    def z_copy(way, d, ch):
        at = part(half_of(d), ch)
        target = same3 if way == 0 else same1
        return copy(same0.at[at], target.at[at], z_s.at[way, d, ch], z_r.at[way, d, ch], to_z[way])

    def z_forward(way, ch):
        at = part(half_of(way), ch)
        source = same3 if way == 0 else same1
        return copy(source.at[at], same2.at[at], zf_s.at[way, ch], zf_r.at[way, ch], to_z[way])

    def core_copy(dz, d, ch):
        at = part(half_of(d), ch)
        return copy(same[dz].at[at], other[dz].at[at], core_s.at[dz, d, ch], core_r.at[dz, d, ch], to_core)

    def each(body):
        def run(ch, carry):
            body(ch)
            return carry

        lax.fori_loop(0, CHUNKS, run, 0)

    pl.semaphore_wait(barrier, 7 + jnp.where(on_ring, 6, 3) + jnp.where(crossed, 1, 0))

    def send_mirrored(ch):
        def pick(n, carry):
            at = ch * step + n
            source = pattern[col, row, lay * half + at]
            mirror_out[at] = stored[jnp.maximum(source, 0)].T
            return carry

        lax.fori_loop(0, step, pick, 0)

        @pl.when(on_ring)
        def _():
            mirror_copy(0, ch, to_crossed).start()
            mirror_copy(1, ch, to_crossed).start()

        @pl.when(jnp.logical_not(on_ring))
        def _():
            @pl.when(crossed)
            def _():
                swap_copy(ch).start()

            @pl.when(jnp.logical_not(crossed))
            def _():
                mirror_copy(0, ch, to_straight).start()

            pass_copy(ch).start()

    @pl.when(off_diagonal)
    def _():
        each(send_mirrored)

    def clear(n, carry):
        out[n] = jnp.zeros(out.shape[1:], out.dtype)
        return carry

    lax.fori_loop(0, half, clear, 0)

    def straight_on(ch):
        swap_copy(ch).wait_recv()
        swap_on(ch).start()

    @pl.when(jnp.logical_and(crossed, jnp.logical_not(on_ring)))
    def _():
        each(straight_on)

    def pass_along(ch):
        for slot in range(3):
            arriving(slot, ch).wait_recv()
            passing_copy(slot, ch).start()

    @pl.when(on_ring)
    def _():
        each(pass_along)

    def complete(ch):
        @pl.when(off_diagonal)
        def _():
            mirror_copy(0, ch, to_straight).wait_recv()
            mirror_copy(1, ch, to_straight).wait_recv()

            def choose(n, carry):
                at = ch * step + n
                r = lay * half + at
                c = jnp.maximum(pattern[row, col, r], 0)
                upper = r * 8 + row <= c * 8 + col
                block = jnp.where(upper, stored[r], mirror_in[at])
                same0[r] = block
                left[0, at] = block
                return carry

            lax.fori_loop(0, step, choose, 0)

        @pl.when(jnp.logical_not(off_diagonal))
        def _():
            def take(n, carry):
                at = ch * step + n
                block = stored[lay * half + at]
                same0[lay * half + at] = block
                left[0, at] = block
                return carry

            lax.fori_loop(0, step, take, 0)

        layer_copy(ch).start()
        for way in range(2):
            x_copy(way, 0, ch).start()
            z_copy(way, 0, ch).start()
        core_copy(0, 0, ch).start()

    each(complete)

    def spread(ch):
        layer_copy(ch).wait_recv()
        y_copy(ch).start()
        for way in range(2):
            z_copy(way, 1, ch).start()
        core_copy(0, 1, ch).start()
        y_copy(ch).wait_recv()
        for way in range(2):
            x_copy(way, 1, ch).start()

    each(spread)

    def forward_first(ch):
        x_copy(0, 0, ch).wait_recv()
        x_forward(0, ch).start()
        z_copy(0, 0, ch).wait_recv()
        z_forward(0, ch).start()
        core_copy(3, 0, ch).start()
        z_copy(1, 0, ch).wait_recv()
        core_copy(1, 0, ch).start()

    each(forward_first)

    def forward_second(ch):
        x_copy(1, 1, ch).wait_recv()
        x_forward(1, ch).start()
        z_copy(1, 1, ch).wait_recv()
        z_forward(1, ch).start()
        core_copy(1, 1, ch).start()
        z_copy(0, 1, ch).wait_recv()
        core_copy(3, 1, ch).start()

    each(forward_second)

    def near(ch):
        x_copy(1, 0, ch).wait_recv()
        x_copy(0, 1, ch).wait_recv()
        for dz in (0, 1, 3):
            for d in range(2):
                core_copy(dz, d, ch).wait_recv()

    each(near)

    def multiply(dz, differs):
        tile = (other if differs else same)[dz]
        m = 2 * ((z + dz) % 4) + (k + differs) % 2
        slot = 2 * ((m // 2 + 4 - x) % 4) + (m % 2 + yh) % 2

        def one(n, carry):
            r = lay * half + n
            c = pattern[row, m, r]
            inner = jnp.maximum(c, 0)
            t = pattern[m, col, inner]
            present = jnp.logical_and(c >= 0, t >= 0)
            block = product(left[slot, n], tile[inner])
            for q in range(2):
                matched = jnp.logical_and(present, wanted[q, r] == t)
                out[n, q] += block * jnp.where(matched, 1.0, 0.0)
            return carry

        lax.fori_loop(0, half, one, 0, unroll=4)

    def far(dz):
        return (z + dz - x + 4) % 4 == 2

    for dz in (0, 1, 3):
        @pl.when(jnp.logical_not(far(dz)))
        def _(dz=dz):
            multiply(dz, 0)
            multiply(dz, 1)

    def last(ch):
        for way in range(2):
            z_forward(way, ch).wait_recv()
            core_copy(2, way, ch).start()
            x_forward(way, ch).wait_recv()

    each(last)

    for dz in (0, 1, 3):
        @pl.when(far(dz))
        def _(dz=dz):
            multiply(dz, 0)
            multiply(dz, 1)

    multiply(2, 0)

    def last_core(ch):
        for d in range(2):
            core_copy(2, d, ch).wait_recv()

    each(last_core)
    multiply(2, 1)

    def drain(ch):
        @pl.when(off_diagonal)
        def _():
            mirror_copy(0, ch, to_straight).wait_send()
            mirror_copy(1, ch, to_straight).wait_send()

        @pl.when(jnp.logical_and(crossed, jnp.logical_not(on_ring)))
        def _():
            swap_on(ch).wait_send()

        @pl.when(on_ring)
        def _():
            for slot in range(3):
                passing_copy(slot, ch).wait_send()

        layer_copy(ch).wait_send()
        y_copy(ch).wait_send()
        for way in range(2):
            x_forward(way, ch).wait_send()
            z_forward(way, ch).wait_send()
            for d in range(2):
                x_copy(way, d, ch).wait_send()
                z_copy(way, d, ch).wait_send()
        for dz in range(4):
            for d in range(2):
                core_copy(dz, d, ch).wait_send()

    each(drain)


def per_device(stored_blocks, pattern, result_cols):
    tile = stored_blocks[0, 0]
    rows, size = tile.shape[0], tile.shape[-1]
    half = rows // 2
    vmem = pl.BlockSpec(memory_space=pltpu.VMEM)
    smem = pl.BlockSpec(memory_space=pltpu.SMEM)
    sems = pltpu.SemaphoreType.DMA
    block = (size, size)
    result = pl.pallas_call(
        functools.partial(kernel, rows),
        out_shape=jax.ShapeDtypeStruct((half, 2, *block), jnp.float32),
        in_specs=[smem, smem, vmem],
        out_specs=vmem,
        scratch_shapes=[
            pltpu.VMEM((half, *block), jnp.float32),
            pltpu.VMEM((half, *block), jnp.float32),
            pltpu.VMEM((half // 2, *block), jnp.float32),
            pltpu.VMEM((3, half // 2, *block), jnp.float32),
            pltpu.VMEM((8, half, *block), jnp.float32),
            *[pltpu.VMEM((rows, *block), jnp.float32)] * 8,
            *[sems((2, CHUNKS))] * 2,
            *[sems((CHUNKS,))] * 2,
            *[sems((3, CHUNKS))] * 2,
            *[sems((CHUNKS,))] * 4,
            *[sems((2, 2, CHUNKS))] * 2,
            *[sems((2, CHUNKS))] * 2,
            *[sems((2, 2, CHUNKS))] * 2,
            *[sems((2, CHUNKS))] * 2,
            *[sems((4, 2, CHUNKS))] * 2,
        ],
        compiler_params=pltpu.CompilerParams(
            collective_id=0, has_side_effects=True, vmem_limit_bytes=58 * 2**20
        ),
    )(pattern, result_cols[0, 0].T, tile)
    return result[None, None]


def solution(mesh):
    return jax.shard_map(
        per_device,
        mesh=mesh,
        in_specs=(P("row", "col", None, None, None), P(), P("row", "col", None, None)),
        out_specs=P("row", "col", "layer", None, None, None),
        check_vma=False,
    )
```

```python
import functools

import jax
import jax.numpy as jnp
from jax import lax
from jax.experimental import pallas as pl
from jax.experimental.pallas import tpu as pltpu
from jax.sharding import PartitionSpec as P

MESH = pl.DeviceIdType.MESH
CHUNKS = 4
SIDE = 0


def product(a, b):
    a_hi = a.astype(jnp.bfloat16)
    a_lo = (a - a_hi.astype(jnp.float32)).astype(jnp.bfloat16)
    b_hi = b.astype(jnp.bfloat16)
    b_lo = (b - b_hi.astype(jnp.float32)).astype(jnp.bfloat16)
    left = jnp.concatenate([a_hi, a_lo, a_hi], axis=1)
    right = jnp.concatenate([b_hi, b_hi, b_lo], axis=0)
    return jnp.dot(left, right, preferred_element_type=jnp.float32)


def kernel(
    rows,
    pattern,
    wanted,
    stored,
    out,
    mirror_out,
    mirror_in,
    swapped,
    passing,
    left,
    same0,
    same1,
    same2,
    same3,
    other0,
    other1,
    other2,
    other3,
    mirror_s,
    mirror_r,
    swap_s,
    swap_r,
    pass_s,
    pass_r,
    layer_s,
    layer_r,
    y_s,
    y_r,
    x_s,
    x_r,
    xf_s,
    xf_r,
    z_s,
    z_r,
    zf_s,
    zf_r,
    core_s,
    core_r,
):
    half = rows // 2
    step = half // CHUNKS
    sub = step // 2
    row = lax.axis_index("row")
    col = lax.axis_index("col")
    lay = lax.axis_index("layer")
    z, k = row // 2, row % 2
    x, yh = col // 2, col % 2
    same = [same0, same1, same2, same3]
    other = [other0, other1, other2, other3]
    on_ring = x == z
    crossed = k != yh
    off_diagonal = jnp.logical_or(jnp.logical_not(on_ring), crossed)

    to_layer = {"layer": 1 - lay}
    to_y = {"col": 2 * x + (1 - yh), "layer": 1 - lay}
    to_core = {"row": 2 * z + (1 - k)}
    to_x = [{"col": (col + 2) % 8}, {"col": (col + 6) % 8}]
    to_z = [{"row": (row + 2) % 8}, {"row": (row + 6) % 8}]
    to_straight = {"row": 2 * x + k, "col": 2 * z + yh}
    to_crossed = {"row": 2 * z + yh, "col": 2 * x + k}
    pass_out = {"row": 2 * x + yh, "col": 2 * x + k}
    pass_in = {"row": row, "col": 2 * z + yh}
    pass_from = [{"row": 2 * ((z + dz) % 4) + yh, "col": 2 * x + k} for dz in (1, 2, 3)]
    pass_on = [{"row": row, "col": 2 * ((z + dz) % 4) + yh} for dz in (1, 2, 3)]
    apart = (x - z + 4) % 4
    near_by = apart % 2 == 1
    far_off = apart == 2
    hop_out = {"row": 2 * ((z + jnp.where(x % 2 == SIDE, 1, 3)) % 4) + yh, "col": 2 * x + k}
    hop_in = {"row": 2 * ((x + jnp.where(z % 2 == SIDE, 1, 3)) % 4) + k, "col": 2 * z + yh}
    hop_from = {"row": 2 * ((x + 2) % 4) + yh, "col": 2 * x + k}
    hop_to = {"row": 2 * x + k, "col": 2 * ((x + 2) % 4) + yh}
    helps = apart == jnp.where(x % 2 == SIDE, 1, 3)

    barrier = pltpu.get_barrier_semaphore()

    def greet(devices):
        for device in devices:
            pl.semaphore_signal(barrier, inc=1, device_id=device, device_id_type=MESH)

    greet([to_layer, to_y, to_core, *to_x, *to_z])

    @pl.when(jnp.logical_and(crossed, jnp.logical_not(far_off)))
    def _():
        greet([to_crossed])

    @pl.when(on_ring)
    def _():
        greet([pass_from[0], pass_from[2], pass_on[0], pass_on[2]])

    @pl.when(near_by)
    def _():
        greet([to_straight, pass_out, pass_in])

    @pl.when(helps)
    def _():
        greet([hop_from, hop_to])

    @pl.when(far_off)
    def _():
        greet([hop_out, hop_in])

    def copy(source, target, send, recv, device):
        return pltpu.make_async_remote_copy(
            src_ref=source,
            dst_ref=target,
            send_sem=send,
            recv_sem=recv,
            device_id=device,
            device_id_type=MESH,
        )

    def part(h, ch):
        return pl.ds(h * half + ch * step, step)

    def piece(ch):
        return pl.ds(ch * step, step)

    def half_of(differs):
        return lay if differs == 0 else 1 - lay

    def mirror_part(p, ch):
        return pl.ds(ch * step + p * sub, sub)

    def mirror_copy(p, ch, device):
        at = mirror_part(p, ch)
        return copy(mirror_out.at[at], mirror_in.at[at], mirror_s.at[p, ch], mirror_r.at[p, ch], device)

    def swap_copy(ch):
        at = pl.ds(ch * sub, sub)
        return copy(mirror_out.at[mirror_part(0, ch)], swapped.at[at], mirror_s.at[0, ch], swap_r.at[ch], to_crossed)

    def swap_on(ch):
        at = pl.ds(ch * sub, sub)
        return copy(swapped.at[at], mirror_in.at[mirror_part(0, ch)], swap_s.at[ch], mirror_r.at[0, ch], to_straight)

    def pass_copy(ch):
        at = pl.ds(ch * sub, sub)
        slot = (z - x + 4) % 4 - 1
        return copy(
            mirror_out.at[mirror_part(1, ch)], passing.at[slot, at], mirror_s.at[1, ch], pass_r.at[slot, ch], pass_out
        )

    def passing_copy(slot, ch):
        at = pl.ds(ch * sub, sub)
        return copy(
            passing.at[slot, at], mirror_in.at[mirror_part(1, ch)], pass_s.at[slot, ch], mirror_r.at[1, ch], pass_on[slot]
        )

    def arriving(slot, ch):
        at = pl.ds(ch * sub, sub)
        return copy(
            mirror_out.at[mirror_part(1, ch)], passing.at[slot, at], mirror_s.at[1, ch], pass_r.at[slot, ch], pass_from[slot]
        )

    def hop_copy(p, ch):
        at = pl.ds(ch * sub, sub)
        return copy(
            mirror_out.at[mirror_part(p, ch)], passing.at[p, at], mirror_s.at[p, ch], pass_r.at[p, ch], hop_out
        )

    def hop_on(p, ch):
        at = pl.ds(ch * sub, sub)
        return copy(
            passing.at[p, at], mirror_in.at[mirror_part(p, ch)], pass_s.at[p, ch], mirror_r.at[p, ch], hop_to
        )

    def layer_copy(ch):
        at = part(lay, ch)
        return copy(same0.at[at], same0.at[at], layer_s.at[ch], layer_r.at[ch], to_layer)

    def y_copy(ch):
        return copy(same0.at[part(1 - lay, ch)], left.at[1, piece(ch)], y_s.at[ch], y_r.at[ch], to_y)

    def x_copy(way, s, ch):
        slot = (6 if way == 0 else 2) + s
        return copy(left.at[s, piece(ch)], left.at[slot, piece(ch)], x_s.at[way, s, ch], x_r.at[way, s, ch], to_x[way])

    def x_forward(way, s, ch):
        slot = (6 if way == 0 else 2) + s
        return copy(left.at[slot, piece(ch)], left.at[4 + s, piece(ch)], xf_s.at[s, ch], xf_r.at[s, ch], to_x[way])

    def z_copy(way, d, ch):
        at = part(half_of(d), ch)
        target = same3 if way == 0 else same1
        return copy(same0.at[at], target.at[at], z_s.at[way, d, ch], z_r.at[way, d, ch], to_z[way])

    def z_forward(way, d, ch):
        at = part(half_of(d), ch)
        source = same3 if way == 0 else same1
        return copy(source.at[at], same2.at[at], zf_s.at[d, ch], zf_r.at[d, ch], to_z[way])

    def one_way(ch, start):
        @pl.when(ch < CHUNKS // 2)
        def _():
            start(0)

        @pl.when(ch >= CHUNKS // 2)
        def _():
            start(1)

    def core_copy(dz, d, ch):
        at = part(half_of(d), ch)
        return copy(same[dz].at[at], other[dz].at[at], core_s.at[dz, d, ch], core_r.at[dz, d, ch], to_core)

    def each(body):
        def run(ch, carry):
            body(ch)
            return carry

        lax.fori_loop(0, CHUNKS, run, 0)

    greeted = jnp.where(on_ring, 4, jnp.where(far_off, 2, 3)) + jnp.where(helps, 2, 0)
    greeted += jnp.where(jnp.logical_and(crossed, jnp.logical_not(far_off)), 1, 0)
    pl.semaphore_wait(barrier, 7 + greeted)

    def send_mirrored(ch):
        def pick(n, carry):
            at = ch * step + n
            source = pattern[col, row, lay * half + at]
            mirror_out[at] = stored[jnp.maximum(source, 0)].T
            return carry

        lax.fori_loop(0, step, pick, 0)

        @pl.when(on_ring)
        def _():
            mirror_copy(0, ch, to_crossed).start()
            mirror_copy(1, ch, to_crossed).start()

        @pl.when(far_off)
        def _():
            hop_copy(0, ch).start()
            hop_copy(1, ch).start()

        @pl.when(near_by)
        def _():
            @pl.when(crossed)
            def _():
                swap_copy(ch).start()

            @pl.when(jnp.logical_not(crossed))
            def _():
                mirror_copy(0, ch, to_straight).start()

            pass_copy(ch).start()

    @pl.when(off_diagonal)
    def _():
        each(send_mirrored)

    def clear(n, carry):
        out[n] = jnp.zeros(out.shape[1:], out.dtype)
        return carry

    lax.fori_loop(0, half, clear, 0)

    def send_on(ch):
        @pl.when(crossed)
        def _():
            swap_copy(ch).wait_recv()
            swap_on(ch).start()

        @pl.when(helps)
        def _():
            for p in range(2):
                hop_copy(p, ch).wait_recv()
                hop_on(p, ch).start()

    @pl.when(near_by)
    def _():
        each(send_on)

    def pass_along(ch):
        for slot in (0, 2):
            arriving(slot, ch).wait_recv()
            passing_copy(slot, ch).start()

    @pl.when(on_ring)
    def _():
        each(pass_along)

    def complete(ch):
        @pl.when(off_diagonal)
        def _():
            mirror_copy(0, ch, to_straight).wait_recv()
            mirror_copy(1, ch, to_straight).wait_recv()

            def choose(n, carry):
                at = ch * step + n
                r = lay * half + at
                c = jnp.maximum(pattern[row, col, r], 0)
                upper = r * 8 + row <= c * 8 + col
                block = jnp.where(upper, stored[r], mirror_in[at])
                same0[r] = block
                left[0, at] = block
                return carry

            lax.fori_loop(0, step, choose, 0)

        @pl.when(jnp.logical_not(off_diagonal))
        def _():
            def take(n, carry):
                at = ch * step + n
                block = stored[lay * half + at]
                same0[lay * half + at] = block
                left[0, at] = block
                return carry

            lax.fori_loop(0, step, take, 0)

        layer_copy(ch).start()
        for way in range(2):
            x_copy(way, 0, ch).start()
            z_copy(way, 0, ch).start()
        core_copy(0, 0, ch).start()

    each(complete)

    def spread_layer(ch):
        layer_copy(ch).wait_recv()
        y_copy(ch).start()
        for way in range(2):
            z_copy(way, 1, ch).start()
        core_copy(0, 1, ch).start()

    each(spread_layer)

    def forward_own(ch):
        for way in range(2):
            x_copy(way, 0, ch).wait_recv()
        one_way(ch, lambda way: x_forward(way, 0, ch).start())
        for way in range(2):
            z_copy(way, 0, ch).wait_recv()
        one_way(ch, lambda way: z_forward(way, 0, ch).start())
        for dz in (1, 3):
            core_copy(dz, 0, ch).start()

    def spread_y(ch):
        y_copy(ch).wait_recv()
        for way in range(2):
            x_copy(way, 1, ch).start()

    each(spread_y)
    each(forward_own)

    def forward_second(ch):
        for way in range(2):
            x_copy(way, 1, ch).wait_recv()
        one_way(ch, lambda way: x_forward(way, 1, ch).start())
        for way in range(2):
            z_copy(way, 1, ch).wait_recv()
        one_way(ch, lambda way: z_forward(way, 1, ch).start())
        for dz in (1, 3):
            core_copy(dz, 1, ch).start()

    each(forward_second)

    def near(ch):
        for dz in (0, 1, 3):
            for d in range(2):
                core_copy(dz, d, ch).wait_recv()

    each(near)

    def multiply(dz, differs):
        tile = (other if differs else same)[dz]
        m = 2 * ((z + dz) % 4) + (k + differs) % 2
        slot = 2 * ((m // 2 + 4 - x) % 4) + (m % 2 + yh) % 2

        def one(n, carry):
            r = lay * half + n
            c = pattern[row, m, r]
            inner = jnp.maximum(c, 0)
            t = pattern[m, col, inner]
            present = jnp.logical_and(c >= 0, t >= 0)
            block = product(left[slot, n], tile[inner])
            for q in range(2):
                matched = jnp.logical_and(present, wanted[q, r] == t)
                out[n, q] += block * jnp.where(matched, 1.0, 0.0)
            return carry

        lax.fori_loop(0, half, one, 0, unroll=4)

    def far(dz):
        return (z + dz - x + 4) % 4 == 2

    for dz in (0, 1, 3):
        @pl.when(jnp.logical_not(far(dz)))
        def _(dz=dz):
            multiply(dz, 0)
            multiply(dz, 1)

    def last(ch):
        for d in range(2):
            z_forward(0, d, ch).wait_recv()
            core_copy(2, d, ch).start()
            x_forward(0, d, ch).wait_recv()

    each(last)

    for dz in (0, 1, 3):
        @pl.when(far(dz))
        def _(dz=dz):
            multiply(dz, 0)
            multiply(dz, 1)

    multiply(2, 0)

    def last_core(ch):
        for d in range(2):
            core_copy(2, d, ch).wait_recv()

    each(last_core)
    multiply(2, 1)

    def drain(ch):
        @pl.when(off_diagonal)
        def _():
            mirror_copy(0, ch, to_straight).wait_send()
            mirror_copy(1, ch, to_straight).wait_send()

        @pl.when(jnp.logical_and(crossed, near_by))
        def _():
            swap_on(ch).wait_send()

        @pl.when(on_ring)
        def _():
            for slot in (0, 2):
                passing_copy(slot, ch).wait_send()

        @pl.when(helps)
        def _():
            for p in range(2):
                hop_on(p, ch).wait_send()

        layer_copy(ch).wait_send()
        y_copy(ch).wait_send()
        for way in range(2):
            x_forward(0, way, ch).wait_send()
            z_forward(0, way, ch).wait_send()
            for d in range(2):
                x_copy(way, d, ch).wait_send()
                z_copy(way, d, ch).wait_send()
        for dz in range(4):
            for d in range(2):
                core_copy(dz, d, ch).wait_send()

    each(drain)


def per_device(stored_blocks, pattern, result_cols):
    tile = stored_blocks[0, 0]
    rows, size = tile.shape[0], tile.shape[-1]
    half = rows // 2
    vmem = pl.BlockSpec(memory_space=pltpu.VMEM)
    smem = pl.BlockSpec(memory_space=pltpu.SMEM)
    sems = pltpu.SemaphoreType.DMA
    block = (size, size)
    result = pl.pallas_call(
        functools.partial(kernel, rows),
        out_shape=jax.ShapeDtypeStruct((half, 2, *block), jnp.float32),
        in_specs=[smem, smem, vmem],
        out_specs=vmem,
        scratch_shapes=[
            pltpu.VMEM((half, *block), jnp.float32),
            pltpu.VMEM((half, *block), jnp.float32),
            pltpu.VMEM((half // 2, *block), jnp.float32),
            pltpu.VMEM((3, half // 2, *block), jnp.float32),
            pltpu.VMEM((8, half, *block), jnp.float32),
            *[pltpu.VMEM((rows, *block), jnp.float32)] * 8,
            *[sems((2, CHUNKS))] * 2,
            *[sems((CHUNKS,))] * 2,
            *[sems((3, CHUNKS))] * 2,
            *[sems((CHUNKS,))] * 4,
            *[sems((2, 2, CHUNKS))] * 2,
            *[sems((2, CHUNKS))] * 2,
            *[sems((2, 2, CHUNKS))] * 2,
            *[sems((2, CHUNKS))] * 2,
            *[sems((4, 2, CHUNKS))] * 2,
        ],
        compiler_params=pltpu.CompilerParams(
            collective_id=0, has_side_effects=True, vmem_limit_bytes=58 * 2**20
        ),
    )(pattern, result_cols[0, 0].T, tile)
    return result[None, None]


def solution(mesh):
    return jax.shard_map(
        per_device,
        mesh=mesh,
        in_specs=(P("row", "col", None, None, None), P(), P("row", "col", None, None)),
        out_specs=P("row", "col", "layer", None, None, None),
        check_vma=False,
    )
```

```python
import functools

import jax
import jax.numpy as jnp
from jax import lax
from jax.experimental import pallas as pl
from jax.experimental.pallas import tpu as pltpu
from jax.sharding import PartitionSpec as P

MESH = pl.DeviceIdType.MESH
CHUNKS = 4
SIDE = 0


def product(a, b):
    a_hi = a.astype(jnp.bfloat16)
    a_lo = (a - a_hi.astype(jnp.float32)).astype(jnp.bfloat16)
    b_hi = b.astype(jnp.bfloat16)
    b_lo = (b - b_hi.astype(jnp.float32)).astype(jnp.bfloat16)
    left = jnp.concatenate([a_hi, a_lo, a_hi], axis=1)
    right = jnp.concatenate([b_hi, b_hi, b_lo], axis=0)
    return jnp.dot(left, right, preferred_element_type=jnp.float32)


def kernel(
    rows,
    pattern,
    wanted,
    stored,
    out,
    mirror_out,
    mirror_in,
    swapped,
    passing,
    left,
    same0,
    same1,
    same2,
    same3,
    other0,
    other1,
    other2,
    other3,
    mirror_s,
    mirror_r,
    swap_s,
    swap_r,
    pass_s,
    pass_r,
    layer_s,
    layer_r,
    y_s,
    y_r,
    x_s,
    x_r,
    pair_s,
    pair_r,
    side_s,
    side_r,
    xf_s,
    xf_r,
    z_s,
    z_r,
    zf_s,
    zf_r,
    core_s,
    core_r,
):
    half = rows // 2
    step = half // CHUNKS
    sub = step // 2
    row = lax.axis_index("row")
    col = lax.axis_index("col")
    lay = lax.axis_index("layer")
    z, k = row // 2, row % 2
    x, yh = col // 2, col % 2
    same = [same0, same1, same2, same3]
    other = [other0, other1, other2, other3]
    on_ring = x == z
    crossed = k != yh
    off_diagonal = jnp.logical_or(jnp.logical_not(on_ring), crossed)

    to_layer = {"layer": 1 - lay}
    to_y = {"col": 2 * x + (1 - yh), "layer": 1 - lay}
    to_pair = {"col": 2 * x + (1 - yh)}
    to_core = {"row": 2 * z + (1 - k)}
    to_x = [{"col": (col + 2) % 8}, {"col": (col + 6) % 8}]
    to_z = [{"row": (row + 2) % 8}, {"row": (row + 6) % 8}]
    to_straight = {"row": 2 * x + k, "col": 2 * z + yh}
    to_crossed = {"row": 2 * z + yh, "col": 2 * x + k}
    pass_out = {"row": 2 * x + yh, "col": 2 * x + k}
    pass_in = {"row": row, "col": 2 * z + yh}
    pass_from = [{"row": 2 * ((z + dz) % 4) + yh, "col": 2 * x + k} for dz in (1, 2, 3)]
    pass_on = [{"row": row, "col": 2 * ((z + dz) % 4) + yh} for dz in (1, 2, 3)]
    apart = (x - z + 4) % 4
    near_by = apart % 2 == 1
    far_off = apart == 2
    hop_out = {"row": 2 * ((z + jnp.where(x % 2 == SIDE, 1, 3)) % 4) + yh, "col": 2 * x + k}
    hop_in = {"row": 2 * ((x + jnp.where(z % 2 == SIDE, 1, 3)) % 4) + k, "col": 2 * z + yh}
    hop_from = {"row": 2 * ((x + 2) % 4) + yh, "col": 2 * x + k}
    hop_to = {"row": 2 * x + k, "col": 2 * ((x + 2) % 4) + yh}
    helps = apart == jnp.where(x % 2 == SIDE, 1, 3)

    barrier = pltpu.get_barrier_semaphore()

    def greet(devices):
        for device in devices:
            pl.semaphore_signal(barrier, inc=1, device_id=device, device_id_type=MESH)

    greet([to_layer, to_y, to_pair, to_core, *to_x, *to_z])

    @pl.when(jnp.logical_and(crossed, jnp.logical_not(far_off)))
    def _():
        greet([to_crossed])

    @pl.when(on_ring)
    def _():
        greet([pass_from[0], pass_from[2], pass_on[0], pass_on[2]])

    @pl.when(near_by)
    def _():
        greet([to_straight, pass_out, pass_in])

    @pl.when(helps)
    def _():
        greet([hop_from, hop_to])

    @pl.when(far_off)
    def _():
        greet([hop_out, hop_in])

    def copy(source, target, send, recv, device):
        return pltpu.make_async_remote_copy(
            src_ref=source,
            dst_ref=target,
            send_sem=send,
            recv_sem=recv,
            device_id=device,
            device_id_type=MESH,
        )

    def part(h, ch):
        return pl.ds(h * half + ch * step, step)

    def piece(ch):
        return pl.ds(ch * step, step)

    def half_of(differs):
        return lay if differs == 0 else 1 - lay

    def mirror_part(p, ch):
        return pl.ds(ch * step + p * sub, sub)

    def mirror_copy(p, ch, device):
        at = mirror_part(p, ch)
        return copy(mirror_out.at[at], mirror_in.at[at], mirror_s.at[p, ch], mirror_r.at[p, ch], device)

    def swap_copy(ch):
        at = pl.ds(ch * sub, sub)
        return copy(mirror_out.at[mirror_part(0, ch)], swapped.at[at], mirror_s.at[0, ch], swap_r.at[ch], to_crossed)

    def swap_on(ch):
        at = pl.ds(ch * sub, sub)
        return copy(swapped.at[at], mirror_in.at[mirror_part(0, ch)], swap_s.at[ch], mirror_r.at[0, ch], to_straight)

    def pass_copy(ch):
        at = pl.ds(ch * sub, sub)
        slot = (z - x + 4) % 4 - 1
        return copy(
            mirror_out.at[mirror_part(1, ch)], passing.at[slot, at], mirror_s.at[1, ch], pass_r.at[slot, ch], pass_out
        )

    def passing_copy(slot, ch):
        at = pl.ds(ch * sub, sub)
        return copy(
            passing.at[slot, at], mirror_in.at[mirror_part(1, ch)], pass_s.at[slot, ch], mirror_r.at[1, ch], pass_on[slot]
        )

    def arriving(slot, ch):
        at = pl.ds(ch * sub, sub)
        return copy(
            mirror_out.at[mirror_part(1, ch)], passing.at[slot, at], mirror_s.at[1, ch], pass_r.at[slot, ch], pass_from[slot]
        )

    def hop_copy(p, ch):
        at = pl.ds(ch * sub, sub)
        return copy(
            mirror_out.at[mirror_part(p, ch)], passing.at[p, at], mirror_s.at[p, ch], pass_r.at[p, ch], hop_out
        )

    def hop_on(p, ch):
        at = pl.ds(ch * sub, sub)
        return copy(
            passing.at[p, at], mirror_in.at[mirror_part(p, ch)], pass_s.at[p, ch], mirror_r.at[p, ch], hop_to
        )

    def layer_copy(ch):
        at = part(lay, ch)
        return copy(same0.at[at], same0.at[at], layer_s.at[ch], layer_r.at[ch], to_layer)

    def y_copy(ch):
        return copy(same0.at[part(1 - lay, ch)], left.at[1, piece(ch)], y_s.at[ch], y_r.at[ch], to_y)

    def x_copy(way, s, ch):
        slot = (6 if way == 0 else 2) + s
        return copy(left.at[s, piece(ch)], left.at[slot, piece(ch)], x_s.at[way, s, ch], x_r.at[way, s, ch], to_x[way])

    aside = (CHUNKS - 1, 0)

    def kept(way, ch, act):
        @pl.when(ch != aside[way])
        def _():
            act()

    def pair_copy(way):
        slot = 6 if way == 0 else 2
        at = piece(aside[way])
        return copy(left.at[slot, at], left.at[slot + 1, at], pair_s.at[way], pair_r.at[way], to_pair)

    def side_copy(way):
        tile = same3 if way == 0 else same1
        at = part(lay, aside[way])
        return copy(tile.at[at], tile.at[at], side_s.at[way], side_r.at[way], to_layer)

    def x_forward(way, s, ch):
        slot = (6 if way == 0 else 2) + s
        return copy(left.at[slot, piece(ch)], left.at[4 + s, piece(ch)], xf_s.at[s, ch], xf_r.at[s, ch], to_x[way])

    def z_copy(way, d, ch):
        at = part(half_of(d), ch)
        target = same3 if way == 0 else same1
        return copy(same0.at[at], target.at[at], z_s.at[way, d, ch], z_r.at[way, d, ch], to_z[way])

    def z_forward(way, d, ch):
        at = part(half_of(d), ch)
        source = same3 if way == 0 else same1
        return copy(source.at[at], same2.at[at], zf_s.at[d, ch], zf_r.at[d, ch], to_z[way])

    def one_way(ch, start):
        @pl.when(ch < CHUNKS // 2)
        def _():
            start(0)

        @pl.when(ch >= CHUNKS // 2)
        def _():
            start(1)

    def core_copy(dz, d, ch):
        at = part(half_of(d), ch)
        return copy(same[dz].at[at], other[dz].at[at], core_s.at[dz, d, ch], core_r.at[dz, d, ch], to_core)

    def each(body):
        def run(ch, carry):
            body(ch)
            return carry

        lax.fori_loop(0, CHUNKS, run, 0)

    greeted = jnp.where(on_ring, 4, jnp.where(far_off, 2, 3)) + jnp.where(helps, 2, 0)
    greeted += jnp.where(jnp.logical_and(crossed, jnp.logical_not(far_off)), 1, 0)
    pl.semaphore_wait(barrier, 8 + greeted)

    def send_mirrored(ch):
        def pick(n, carry):
            at = ch * step + n
            source = pattern[col, row, lay * half + at]
            mirror_out[at] = stored[jnp.maximum(source, 0)].T
            return carry

        lax.fori_loop(0, step, pick, 0)

        @pl.when(on_ring)
        def _():
            mirror_copy(0, ch, to_crossed).start()
            mirror_copy(1, ch, to_crossed).start()

        @pl.when(far_off)
        def _():
            hop_copy(0, ch).start()
            hop_copy(1, ch).start()

        @pl.when(near_by)
        def _():
            @pl.when(crossed)
            def _():
                swap_copy(ch).start()

            @pl.when(jnp.logical_not(crossed))
            def _():
                mirror_copy(0, ch, to_straight).start()

            pass_copy(ch).start()

    @pl.when(off_diagonal)
    def _():
        each(send_mirrored)

    def clear(n, carry):
        out[n] = jnp.zeros(out.shape[1:], out.dtype)
        return carry

    lax.fori_loop(0, half, clear, 0)

    def send_on(ch):
        @pl.when(crossed)
        def _():
            swap_copy(ch).wait_recv()
            swap_on(ch).start()

        @pl.when(helps)
        def _():
            for p in range(2):
                hop_copy(p, ch).wait_recv()
                hop_on(p, ch).start()

    @pl.when(near_by)
    def _():
        each(send_on)

    def pass_along(ch):
        for slot in (0, 2):
            arriving(slot, ch).wait_recv()
            passing_copy(slot, ch).start()

    @pl.when(on_ring)
    def _():
        each(pass_along)

    def complete(ch):
        @pl.when(off_diagonal)
        def _():
            mirror_copy(0, ch, to_straight).wait_recv()
            mirror_copy(1, ch, to_straight).wait_recv()

            def choose(n, carry):
                at = ch * step + n
                r = lay * half + at
                c = jnp.maximum(pattern[row, col, r], 0)
                upper = r * 8 + row <= c * 8 + col
                block = jnp.where(upper, stored[r], mirror_in[at])
                same0[r] = block
                left[0, at] = block
                return carry

            lax.fori_loop(0, step, choose, 0)

        @pl.when(jnp.logical_not(off_diagonal))
        def _():
            def take(n, carry):
                at = ch * step + n
                block = stored[lay * half + at]
                same0[lay * half + at] = block
                left[0, at] = block
                return carry

            lax.fori_loop(0, step, take, 0)

        layer_copy(ch).start()
        for way in range(2):
            x_copy(way, 0, ch).start()
            z_copy(way, 0, ch).start()
        core_copy(0, 0, ch).start()

    each(complete)

    def spread_layer(ch):
        layer_copy(ch).wait_recv()
        y_copy(ch).start()
        for way in range(2):
            kept(way, ch, z_copy(way, 1, ch).start)
        core_copy(0, 1, ch).start()

    each(spread_layer)

    def forward_own(ch):
        for way in range(2):
            x_copy(way, 0, ch).wait_recv()
        one_way(ch, lambda way: x_forward(way, 0, ch).start())
        for way in range(2):
            z_copy(way, 0, ch).wait_recv()
        one_way(ch, lambda way: z_forward(way, 0, ch).start())
        for dz in (1, 3):
            core_copy(dz, 0, ch).start()
        for way in range(2):
            @pl.when(ch == aside[way])
            def _(way=way):
                side_copy(way).start()
                pair_copy(way).start()

    def spread_y(ch):
        y_copy(ch).wait_recv()
        for way in range(2):
            kept(way, ch, x_copy(way, 1, ch).start)

    each(spread_y)
    each(forward_own)

    def forward_second(ch):
        for way in range(2):
            kept(way, ch, x_copy(way, 1, ch).wait_recv)
        one_way(ch, lambda way: x_forward(way, 1, ch).start())
        for way in range(2):
            kept(way, ch, z_copy(way, 1, ch).wait_recv)
        one_way(ch, lambda way: z_forward(way, 1, ch).start())
        for way, dz in ((0, 3), (1, 1)):
            kept(way, ch, core_copy(dz, 1, ch).start)

    each(forward_second)
    for way, dz in ((0, 3), (1, 1)):
        side_copy(way).wait_recv()
        core_copy(dz, 1, aside[way]).start()
        pair_copy(way).wait_recv()

    def near(ch):
        for dz in (0, 1, 3):
            for d in range(2):
                core_copy(dz, d, ch).wait_recv()

    each(near)

    def multiply(dz, differs):
        tile = (other if differs else same)[dz]
        m = 2 * ((z + dz) % 4) + (k + differs) % 2
        slot = 2 * ((m // 2 + 4 - x) % 4) + (m % 2 + yh) % 2

        def one(n, carry):
            r = lay * half + n
            c = pattern[row, m, r]
            inner = jnp.maximum(c, 0)
            t = pattern[m, col, inner]
            present = jnp.logical_and(c >= 0, t >= 0)
            block = product(left[slot, n], tile[inner])
            for q in range(2):
                matched = jnp.logical_and(present, wanted[q, r] == t)
                out[n, q] += block * jnp.where(matched, 1.0, 0.0)
            return carry

        lax.fori_loop(0, half, one, 0, unroll=4)

    def far(dz):
        return (z + dz - x + 4) % 4 == 2

    for dz in (0, 1, 3):
        @pl.when(jnp.logical_not(far(dz)))
        def _(dz=dz):
            multiply(dz, 0)
            multiply(dz, 1)

    def last(ch):
        for d in range(2):
            z_forward(0, d, ch).wait_recv()
            core_copy(2, d, ch).start()
            x_forward(0, d, ch).wait_recv()

    each(last)

    for dz in (0, 1, 3):
        @pl.when(far(dz))
        def _(dz=dz):
            multiply(dz, 0)
            multiply(dz, 1)

    multiply(2, 0)

    def last_core(ch):
        for d in range(2):
            core_copy(2, d, ch).wait_recv()

    each(last_core)
    multiply(2, 1)

    def drain(ch):
        @pl.when(off_diagonal)
        def _():
            mirror_copy(0, ch, to_straight).wait_send()
            mirror_copy(1, ch, to_straight).wait_send()

        @pl.when(jnp.logical_and(crossed, near_by))
        def _():
            swap_on(ch).wait_send()

        @pl.when(on_ring)
        def _():
            for slot in (0, 2):
                passing_copy(slot, ch).wait_send()

        @pl.when(helps)
        def _():
            for p in range(2):
                hop_on(p, ch).wait_send()

        layer_copy(ch).wait_send()
        y_copy(ch).wait_send()
        for way in range(2):
            x_forward(0, way, ch).wait_send()
            z_forward(0, way, ch).wait_send()
            x_copy(way, 0, ch).wait_send()
            z_copy(way, 0, ch).wait_send()
            kept(way, ch, x_copy(way, 1, ch).wait_send)
            kept(way, ch, z_copy(way, 1, ch).wait_send)
        for dz in range(4):
            for d in range(2):
                core_copy(dz, d, ch).wait_send()

    each(drain)
    for way in range(2):
        side_copy(way).wait_send()
        pair_copy(way).wait_send()


def per_device(stored_blocks, pattern, result_cols):
    tile = stored_blocks[0, 0]
    rows, size = tile.shape[0], tile.shape[-1]
    half = rows // 2
    vmem = pl.BlockSpec(memory_space=pltpu.VMEM)
    smem = pl.BlockSpec(memory_space=pltpu.SMEM)
    sems = pltpu.SemaphoreType.DMA
    block = (size, size)
    result = pl.pallas_call(
        functools.partial(kernel, rows),
        out_shape=jax.ShapeDtypeStruct((half, 2, *block), jnp.float32),
        in_specs=[smem, smem, vmem],
        out_specs=vmem,
        scratch_shapes=[
            pltpu.VMEM((half, *block), jnp.float32),
            pltpu.VMEM((half, *block), jnp.float32),
            pltpu.VMEM((half // 2, *block), jnp.float32),
            pltpu.VMEM((3, half // 2, *block), jnp.float32),
            pltpu.VMEM((8, half, *block), jnp.float32),
            *[pltpu.VMEM((rows, *block), jnp.float32)] * 8,
            *[sems((2, CHUNKS))] * 2,
            *[sems((CHUNKS,))] * 2,
            *[sems((3, CHUNKS))] * 2,
            *[sems((CHUNKS,))] * 4,
            *[sems((2, 2, CHUNKS))] * 2,
            *[sems((2,))] * 4,
            *[sems((2, CHUNKS))] * 2,
            *[sems((2, 2, CHUNKS))] * 2,
            *[sems((2, CHUNKS))] * 2,
            *[sems((4, 2, CHUNKS))] * 2,
        ],
        compiler_params=pltpu.CompilerParams(
            collective_id=0, has_side_effects=True, vmem_limit_bytes=58 * 2**20
        ),
    )(pattern, result_cols[0, 0].T, tile)
    return result[None, None]


def solution(mesh):
    return jax.shard_map(
        per_device,
        mesh=mesh,
        in_specs=(P("row", "col", None, None, None), P(), P("row", "col", None, None)),
        out_specs=P("row", "col", "layer", None, None, None),
        check_vma=False,
    )
```

```python
import functools

import jax
import jax.numpy as jnp
from jax import lax
from jax.experimental import pallas as pl
from jax.experimental.pallas import tpu as pltpu
from jax.sharding import PartitionSpec as P

MESH = pl.DeviceIdType.MESH
CHUNKS = 6
ASIDE = 2
SIDE = 0


def product(a, b):
    a_hi = a.astype(jnp.bfloat16)
    a_lo = (a - a_hi.astype(jnp.float32)).astype(jnp.bfloat16)
    b_hi = b.astype(jnp.bfloat16)
    b_lo = (b - b_hi.astype(jnp.float32)).astype(jnp.bfloat16)
    left = jnp.concatenate([a_hi, a_lo, a_hi], axis=1)
    right = jnp.concatenate([b_hi, b_hi, b_lo], axis=0)
    return jnp.dot(left, right, preferred_element_type=jnp.float32)


def kernel(
    rows,
    pattern,
    wanted,
    stored_hbm,
    out,
    stored,
    stored_sem,
    mirror_out,
    mirror_in,
    swapped,
    passing,
    left,
    same0,
    same1,
    same2,
    same3,
    other0,
    other1,
    other2,
    other3,
    mirror_s,
    mirror_r,
    swap_s,
    swap_r,
    pass_s,
    pass_r,
    layer_s,
    layer_r,
    y_s,
    y_r,
    x_s,
    x_r,
    pair_s,
    pair_r,
    side_s,
    side_r,
    xf_s,
    xf_r,
    z_s,
    z_r,
    zf_s,
    zf_r,
    core_s,
    core_r,
):
    half = rows // 2
    step = half // CHUNKS
    sub = step // 2
    row = lax.axis_index("row")
    col = lax.axis_index("col")
    lay = lax.axis_index("layer")
    z, k = row // 2, row % 2
    x, yh = col // 2, col % 2
    same = [same0, same1, same2, same3]
    other = [other0, other1, other2, other3]
    on_ring = x == z
    crossed = k != yh
    off_diagonal = jnp.logical_or(jnp.logical_not(on_ring), crossed)

    to_layer = {"layer": 1 - lay}
    to_y = {"col": 2 * x + (1 - yh), "layer": 1 - lay}
    to_pair = {"col": 2 * x + (1 - yh)}
    to_core = {"row": 2 * z + (1 - k)}
    to_x = [{"col": (col + 2) % 8}, {"col": (col + 6) % 8}]
    to_z = [{"row": (row + 2) % 8}, {"row": (row + 6) % 8}]
    to_straight = {"row": 2 * x + k, "col": 2 * z + yh}
    to_crossed = {"row": 2 * z + yh, "col": 2 * x + k}
    pass_out = {"row": 2 * x + yh, "col": 2 * x + k}
    pass_in = {"row": row, "col": 2 * z + yh}
    pass_from = [{"row": 2 * ((z + dz) % 4) + yh, "col": 2 * x + k} for dz in (1, 2, 3)]
    pass_on = [{"row": row, "col": 2 * ((z + dz) % 4) + yh} for dz in (1, 2, 3)]
    apart = (x - z + 4) % 4
    near_by = apart % 2 == 1
    far_off = apart == 2
    hop_out = {"row": 2 * ((z + jnp.where(x % 2 == SIDE, 1, 3)) % 4) + yh, "col": 2 * x + k}
    hop_in = {"row": 2 * ((x + jnp.where(z % 2 == SIDE, 1, 3)) % 4) + k, "col": 2 * z + yh}
    hop_from = {"row": 2 * ((x + 2) % 4) + yh, "col": 2 * x + k}
    hop_to = {"row": 2 * x + k, "col": 2 * ((x + 2) % 4) + yh}
    helps = apart == jnp.where(x % 2 == SIDE, 1, 3)

    load = pltpu.make_async_copy(stored_hbm, stored, stored_sem)
    load.start()
    barrier = pltpu.get_barrier_semaphore()

    def greet(devices):
        for device in devices:
            pl.semaphore_signal(barrier, inc=1, device_id=device, device_id_type=MESH)

    greet([to_layer, to_y, to_pair, to_core, *to_x, *to_z])

    @pl.when(jnp.logical_and(crossed, jnp.logical_not(far_off)))
    def _():
        greet([to_crossed])

    @pl.when(on_ring)
    def _():
        greet([pass_from[0], pass_from[2], pass_on[0], pass_on[2]])

    @pl.when(near_by)
    def _():
        greet([to_straight, pass_out, pass_in])

    @pl.when(helps)
    def _():
        greet([hop_from, hop_to])

    @pl.when(far_off)
    def _():
        greet([hop_out, hop_in])

    def copy(source, target, send, recv, device):
        return pltpu.make_async_remote_copy(
            src_ref=source,
            dst_ref=target,
            send_sem=send,
            recv_sem=recv,
            device_id=device,
            device_id_type=MESH,
        )

    def part(h, ch):
        return pl.ds(h * half + ch * step, step)

    def piece(ch):
        return pl.ds(ch * step, step)

    def half_of(differs):
        return lay if differs == 0 else 1 - lay

    def mirror_part(p, ch):
        return pl.ds(ch * step + p * sub, sub)

    def mirror_copy(p, ch, device):
        at = mirror_part(p, ch)
        return copy(mirror_out.at[at], mirror_in.at[at], mirror_s.at[p, ch], mirror_r.at[p, ch], device)

    def swap_copy(ch):
        at = pl.ds(ch * sub, sub)
        return copy(mirror_out.at[mirror_part(0, ch)], swapped.at[at], mirror_s.at[0, ch], swap_r.at[ch], to_crossed)

    def swap_on(ch):
        at = pl.ds(ch * sub, sub)
        return copy(swapped.at[at], mirror_in.at[mirror_part(0, ch)], swap_s.at[ch], mirror_r.at[0, ch], to_straight)

    def pass_copy(ch):
        at = pl.ds(ch * sub, sub)
        slot = (z - x + 4) % 4 - 1
        return copy(
            mirror_out.at[mirror_part(1, ch)], passing.at[slot, at], mirror_s.at[1, ch], pass_r.at[slot, ch], pass_out
        )

    def passing_copy(slot, ch):
        at = pl.ds(ch * sub, sub)
        return copy(
            passing.at[slot, at], mirror_in.at[mirror_part(1, ch)], pass_s.at[slot, ch], mirror_r.at[1, ch], pass_on[slot]
        )

    def arriving(slot, ch):
        at = pl.ds(ch * sub, sub)
        return copy(
            mirror_out.at[mirror_part(1, ch)], passing.at[slot, at], mirror_s.at[1, ch], pass_r.at[slot, ch], pass_from[slot]
        )

    def hop_copy(p, ch):
        at = pl.ds(ch * sub, sub)
        return copy(
            mirror_out.at[mirror_part(p, ch)], passing.at[p, at], mirror_s.at[p, ch], pass_r.at[p, ch], hop_out
        )

    def hop_on(p, ch):
        at = pl.ds(ch * sub, sub)
        return copy(
            passing.at[p, at], mirror_in.at[mirror_part(p, ch)], pass_s.at[p, ch], mirror_r.at[p, ch], hop_to
        )

    def layer_copy(ch):
        at = part(lay, ch)
        return copy(same0.at[at], same0.at[at], layer_s.at[ch], layer_r.at[ch], to_layer)

    def y_copy(ch):
        return copy(same0.at[part(1 - lay, ch)], left.at[1, piece(ch)], y_s.at[ch], y_r.at[ch], to_y)

    def x_copy(way, s, ch):
        slot = (6 if way == 0 else 2) + s
        return copy(left.at[s, piece(ch)], left.at[slot, piece(ch)], x_s.at[way, s, ch], x_r.at[way, s, ch], to_x[way])

    aside = (CHUNKS - ASIDE, 0)

    def kept(way, ch, act):
        @pl.when(ch < aside[0] if way == 0 else ch >= ASIDE)
        def _():
            act()

    def pair_copy(way):
        slot = 6 if way == 0 else 2
        at = pl.ds(aside[way] * step, ASIDE * step)
        return copy(left.at[slot, at], left.at[slot + 1, at], pair_s.at[way], pair_r.at[way], to_pair)

    def side_copy(way):
        tile = same3 if way == 0 else same1
        at = pl.ds(lay * half + aside[way] * step, ASIDE * step)
        return copy(tile.at[at], tile.at[at], side_s.at[way], side_r.at[way], to_layer)

    def x_forward(way, s, ch):
        slot = (6 if way == 0 else 2) + s
        return copy(left.at[slot, piece(ch)], left.at[4 + s, piece(ch)], xf_s.at[s, ch], xf_r.at[s, ch], to_x[way])

    def z_copy(way, d, ch):
        at = part(half_of(d), ch)
        target = same3 if way == 0 else same1
        return copy(same0.at[at], target.at[at], z_s.at[way, d, ch], z_r.at[way, d, ch], to_z[way])

    def z_forward(way, d, ch):
        at = part(half_of(d), ch)
        source = same3 if way == 0 else same1
        return copy(source.at[at], same2.at[at], zf_s.at[d, ch], zf_r.at[d, ch], to_z[way])

    def one_way(ch, start):
        @pl.when(ch < CHUNKS // 2)
        def _():
            start(0)

        @pl.when(ch >= CHUNKS // 2)
        def _():
            start(1)

    def core_copy(dz, d, ch):
        at = part(half_of(d), ch)
        return copy(same[dz].at[at], other[dz].at[at], core_s.at[dz, d, ch], core_r.at[dz, d, ch], to_core)

    def each(body):
        def run(ch, carry):
            body(ch)
            return carry

        lax.fori_loop(0, CHUNKS, run, 0)

    greeted = jnp.where(on_ring, 4, jnp.where(far_off, 2, 3)) + jnp.where(helps, 2, 0)
    greeted += jnp.where(jnp.logical_and(crossed, jnp.logical_not(far_off)), 1, 0)
    pl.semaphore_wait(barrier, 8 + greeted)

    load.wait()

    def send_mirrored(ch):
        def pick(n, carry):
            at = ch * step + n
            source = pattern[col, row, lay * half + at]
            mirror_out[at] = stored[jnp.maximum(source, 0)].T
            return carry

        lax.fori_loop(0, step, pick, 0)

        @pl.when(on_ring)
        def _():
            mirror_copy(0, ch, to_crossed).start()
            mirror_copy(1, ch, to_crossed).start()

        @pl.when(far_off)
        def _():
            hop_copy(0, ch).start()
            hop_copy(1, ch).start()

        @pl.when(near_by)
        def _():
            @pl.when(crossed)
            def _():
                swap_copy(ch).start()

            @pl.when(jnp.logical_not(crossed))
            def _():
                mirror_copy(0, ch, to_straight).start()

            pass_copy(ch).start()

    @pl.when(off_diagonal)
    def _():
        each(send_mirrored)

    def clear(n, carry):
        out[n] = jnp.zeros(out.shape[1:], out.dtype)
        return carry

    lax.fori_loop(0, half, clear, 0)

    def send_on(ch):
        @pl.when(crossed)
        def _():
            swap_copy(ch).wait_recv()
            swap_on(ch).start()

        @pl.when(helps)
        def _():
            for p in range(2):
                hop_copy(p, ch).wait_recv()
                hop_on(p, ch).start()

    @pl.when(near_by)
    def _():
        each(send_on)

    def pass_along(ch):
        for slot in (0, 2):
            arriving(slot, ch).wait_recv()
            passing_copy(slot, ch).start()

    @pl.when(on_ring)
    def _():
        each(pass_along)

    def complete(ch):
        @pl.when(off_diagonal)
        def _():
            mirror_copy(0, ch, to_straight).wait_recv()
            mirror_copy(1, ch, to_straight).wait_recv()

            def choose(n, carry):
                at = ch * step + n
                r = lay * half + at
                c = jnp.maximum(pattern[row, col, r], 0)
                upper = r * 8 + row <= c * 8 + col
                block = jnp.where(upper, stored[r], mirror_in[at])
                same0[r] = block
                left[0, at] = block
                return carry

            lax.fori_loop(0, step, choose, 0)

        @pl.when(jnp.logical_not(off_diagonal))
        def _():
            def take(n, carry):
                at = ch * step + n
                block = stored[lay * half + at]
                same0[lay * half + at] = block
                left[0, at] = block
                return carry

            lax.fori_loop(0, step, take, 0)

        layer_copy(ch).start()
        for way in range(2):
            x_copy(way, 0, ch).start()
            z_copy(way, 0, ch).start()
        core_copy(0, 0, ch).start()

    each(complete)

    def spread_layer(ch):
        layer_copy(ch).wait_recv()
        y_copy(ch).start()
        for way in range(2):
            kept(way, ch, z_copy(way, 1, ch).start)
        core_copy(0, 1, ch).start()

    each(spread_layer)

    def forward_own(ch):
        for way in range(2):
            x_copy(way, 0, ch).wait_recv()
        one_way(ch, lambda way: x_forward(way, 0, ch).start())
        for way in range(2):
            z_copy(way, 0, ch).wait_recv()
        one_way(ch, lambda way: z_forward(way, 0, ch).start())
        for dz in (1, 3):
            core_copy(dz, 0, ch).start()
        for way in range(2):
            @pl.when(ch == aside[way] + ASIDE - 1)
            def _(way=way):
                side_copy(way).start()
                pair_copy(way).start()

    def spread_y(ch):
        y_copy(ch).wait_recv()
        for way in range(2):
            kept(way, ch, x_copy(way, 1, ch).start)

    each(spread_y)
    each(forward_own)

    def forward_second(ch):
        for way in range(2):
            kept(way, ch, x_copy(way, 1, ch).wait_recv)
        one_way(ch, lambda way: x_forward(way, 1, ch).start())
        for way in range(2):
            kept(way, ch, z_copy(way, 1, ch).wait_recv)
        one_way(ch, lambda way: z_forward(way, 1, ch).start())
        for way, dz in ((0, 3), (1, 1)):
            kept(way, ch, core_copy(dz, 1, ch).start)

    each(forward_second)
    for way, dz in ((0, 3), (1, 1)):
        side_copy(way).wait_recv()
        for n in range(ASIDE):
            core_copy(dz, 1, aside[way] + n).start()
        pair_copy(way).wait_recv()

    def near(ch):
        for dz in (0, 1, 3):
            for d in range(2):
                core_copy(dz, d, ch).wait_recv()

    each(near)

    def multiply(dz, differs):
        tile = (other if differs else same)[dz]
        m = 2 * ((z + dz) % 4) + (k + differs) % 2
        slot = 2 * ((m // 2 + 4 - x) % 4) + (m % 2 + yh) % 2

        def one(n, carry):
            r = lay * half + n
            c = pattern[row, m, r]
            inner = jnp.maximum(c, 0)
            t = pattern[m, col, inner]
            present = jnp.logical_and(c >= 0, t >= 0)
            block = product(left[slot, n], tile[inner])
            for q in range(2):
                matched = jnp.logical_and(present, wanted[q, r] == t)
                out[n, q] += block * jnp.where(matched, 1.0, 0.0)
            return carry

        lax.fori_loop(0, half, one, 0, unroll=8)

    def far(dz):
        return (z + dz - x + 4) % 4 == 2

    for dz in (0, 1, 3):
        @pl.when(jnp.logical_not(far(dz)))
        def _(dz=dz):
            multiply(dz, 0)
            multiply(dz, 1)

    def last(ch):
        for d in range(2):
            z_forward(0, d, ch).wait_recv()
            core_copy(2, d, ch).start()
            x_forward(0, d, ch).wait_recv()

    each(last)

    for dz in (0, 1, 3):
        @pl.when(far(dz))
        def _(dz=dz):
            multiply(dz, 0)
            multiply(dz, 1)

    multiply(2, 0)

    def last_core(ch):
        for d in range(2):
            core_copy(2, d, ch).wait_recv()

    each(last_core)
    multiply(2, 1)

    def drain(ch):
        @pl.when(off_diagonal)
        def _():
            mirror_copy(0, ch, to_straight).wait_send()
            mirror_copy(1, ch, to_straight).wait_send()

        @pl.when(jnp.logical_and(crossed, near_by))
        def _():
            swap_on(ch).wait_send()

        @pl.when(on_ring)
        def _():
            for slot in (0, 2):
                passing_copy(slot, ch).wait_send()

        @pl.when(helps)
        def _():
            for p in range(2):
                hop_on(p, ch).wait_send()

        layer_copy(ch).wait_send()
        y_copy(ch).wait_send()
        for way in range(2):
            x_forward(0, way, ch).wait_send()
            z_forward(0, way, ch).wait_send()
            x_copy(way, 0, ch).wait_send()
            z_copy(way, 0, ch).wait_send()
            kept(way, ch, x_copy(way, 1, ch).wait_send)
            kept(way, ch, z_copy(way, 1, ch).wait_send)
        for dz in range(4):
            for d in range(2):
                core_copy(dz, d, ch).wait_send()

    each(drain)
    for way in range(2):
        side_copy(way).wait_send()
        pair_copy(way).wait_send()


def per_device(stored_blocks, pattern, result_cols):
    tile = stored_blocks[0, 0]
    rows, size = tile.shape[0], tile.shape[-1]
    half = rows // 2
    vmem = pl.BlockSpec(memory_space=pltpu.VMEM)
    smem = pl.BlockSpec(memory_space=pltpu.SMEM)
    sems = pltpu.SemaphoreType.DMA
    block = (size, size)
    result = pl.pallas_call(
        functools.partial(kernel, rows),
        out_shape=jax.ShapeDtypeStruct((half, 2, *block), jnp.float32),
        in_specs=[smem, smem, pl.BlockSpec(memory_space=pl.ANY)],
        out_specs=vmem,
        scratch_shapes=[
            pltpu.VMEM((rows, *block), jnp.float32),
            sems(()),
            pltpu.VMEM((half, *block), jnp.float32),
            pltpu.VMEM((half, *block), jnp.float32),
            pltpu.VMEM((half // 2, *block), jnp.float32),
            pltpu.VMEM((3, half // 2, *block), jnp.float32),
            pltpu.VMEM((8, half, *block), jnp.float32),
            *[pltpu.VMEM((rows, *block), jnp.float32)] * 8,
            *[sems((2, CHUNKS))] * 2,
            *[sems((CHUNKS,))] * 2,
            *[sems((3, CHUNKS))] * 2,
            *[sems((CHUNKS,))] * 4,
            *[sems((2, 2, CHUNKS))] * 2,
            *[sems((2,))] * 4,
            *[sems((2, CHUNKS))] * 2,
            *[sems((2, 2, CHUNKS))] * 2,
            *[sems((2, CHUNKS))] * 2,
            *[sems((4, 2, CHUNKS))] * 2,
        ],
        compiler_params=pltpu.CompilerParams(
            collective_id=0, has_side_effects=True, vmem_limit_bytes=58 * 2**20
        ),
    )(pattern, result_cols[0, 0].T, tile)
    return result[None, None]


def solution(mesh):
    return jax.shard_map(
        per_device,
        mesh=mesh,
        in_specs=(P("row", "col", None, None, None), P(), P("row", "col", None, None)),
        out_specs=P("row", "col", "layer", None, None, None),
        check_vma=False,
    )
```

```python
import functools

import jax
import jax.numpy as jnp
from jax import lax
from jax.experimental import pallas as pl
from jax.experimental.pallas import tpu as pltpu
from jax.sharding import PartitionSpec as P

MESH = pl.DeviceIdType.MESH
CHUNKS = 6
ASIDE = 2
DIRECT = 2
SIDE = 0


def product(a, b):
    a_hi = a.astype(jnp.bfloat16)
    a_lo = (a - a_hi.astype(jnp.float32)).astype(jnp.bfloat16)
    b_hi = b.astype(jnp.bfloat16)
    b_lo = (b - b_hi.astype(jnp.float32)).astype(jnp.bfloat16)
    left = jnp.concatenate([a_hi, a_lo, a_hi], axis=1)
    right = jnp.concatenate([b_hi, b_hi, b_lo], axis=0)
    return jnp.dot(left, right, preferred_element_type=jnp.float32)


def kernel(
    rows,
    pattern,
    wanted,
    stored_hbm,
    out,
    stored,
    stored_sem,
    mirror_out,
    mirror_in,
    swapped,
    passing,
    left,
    same0,
    same1,
    same2,
    same3,
    other0,
    other1,
    other2,
    other3,
    mirror_s,
    mirror_r,
    swap_s,
    swap_r,
    pass_s,
    pass_r,
    layer_s,
    layer_r,
    y_s,
    y_r,
    x_s,
    x_r,
    pair_s,
    pair_r,
    side_s,
    side_r,
    xf_s,
    xf_r,
    z_s,
    z_r,
    zf_s,
    zf_r,
    core_s,
    core_r,
):
    half = rows // 2
    step = half // CHUNKS
    sub = step // 2
    row = lax.axis_index("row")
    col = lax.axis_index("col")
    lay = lax.axis_index("layer")
    z, k = row // 2, row % 2
    x, yh = col // 2, col % 2
    same = [same0, same1, same2, same3]
    other = [other0, other1, other2, other3]
    on_ring = x == z
    crossed = k != yh
    off_diagonal = jnp.logical_or(jnp.logical_not(on_ring), crossed)

    to_layer = {"layer": 1 - lay}
    to_y = {"col": 2 * x + (1 - yh), "layer": 1 - lay}
    to_pair = {"col": 2 * x + (1 - yh)}
    to_core = {"row": 2 * z + (1 - k)}
    to_x = [{"col": (col + 2) % 8}, {"col": (col + 6) % 8}]
    to_z = [{"row": (row + 2) % 8}, {"row": (row + 6) % 8}]
    to_straight = {"row": 2 * x + k, "col": 2 * z + yh}
    to_crossed = {"row": 2 * z + yh, "col": 2 * x + k}
    pass_out = {"row": 2 * x + yh, "col": 2 * x + k}
    pass_in = {"row": row, "col": 2 * z + yh}
    pass_from = [{"row": 2 * ((z + dz) % 4) + yh, "col": 2 * x + k} for dz in (1, 2, 3)]
    pass_on = [{"row": row, "col": 2 * ((z + dz) % 4) + yh} for dz in (1, 2, 3)]
    apart = (x - z + 4) % 4
    near_by = apart % 2 == 1
    far_off = apart == 2
    to_mirror = {"row": col, "col": row}
    hop_out = {"row": 2 * ((z + jnp.where(x % 2 == SIDE, 1, 3)) % 4) + yh, "col": 2 * x + k}
    hop_in = {"row": 2 * ((x + jnp.where(z % 2 == SIDE, 1, 3)) % 4) + k, "col": 2 * z + yh}
    hop_from = {"row": 2 * ((x + 2) % 4) + yh, "col": 2 * x + k}
    hop_to = {"row": 2 * x + k, "col": 2 * ((x + 2) % 4) + yh}
    helps = apart == jnp.where(x % 2 == SIDE, 1, 3)

    load = pltpu.make_async_copy(stored_hbm, stored, stored_sem)
    load.start()
    barrier = pltpu.get_barrier_semaphore()

    def greet(devices):
        for device in devices:
            pl.semaphore_signal(barrier, inc=1, device_id=device, device_id_type=MESH)

    greet([to_layer, to_y, to_pair, to_core, *to_x, *to_z])

    @pl.when(jnp.logical_and(crossed, jnp.logical_not(far_off)))
    def _():
        greet([to_crossed])

    @pl.when(on_ring)
    def _():
        greet([pass_from[0], pass_from[2], pass_on[0], pass_on[2]])

    @pl.when(near_by)
    def _():
        greet([to_straight, pass_out, pass_in])

    @pl.when(helps)
    def _():
        greet([hop_from, hop_to])

    @pl.when(far_off)
    def _():
        greet([hop_out, hop_in, to_mirror])

    def copy(source, target, send, recv, device):
        return pltpu.make_async_remote_copy(
            src_ref=source,
            dst_ref=target,
            send_sem=send,
            recv_sem=recv,
            device_id=device,
            device_id_type=MESH,
        )

    def part(h, ch):
        return pl.ds(h * half + ch * step, step)

    def piece(ch):
        return pl.ds(ch * step, step)

    def half_of(differs):
        return lay if differs == 0 else 1 - lay

    def mirror_part(p, ch):
        return pl.ds(ch * step + p * sub, sub)

    def mirror_copy(p, ch, device):
        at = mirror_part(p, ch)
        return copy(mirror_out.at[at], mirror_in.at[at], mirror_s.at[p, ch], mirror_r.at[p, ch], device)

    def swap_copy(ch):
        at = pl.ds(ch * sub, sub)
        return copy(mirror_out.at[mirror_part(0, ch)], swapped.at[at], mirror_s.at[0, ch], swap_r.at[ch], to_crossed)

    def swap_on(ch):
        at = pl.ds(ch * sub, sub)
        return copy(swapped.at[at], mirror_in.at[mirror_part(0, ch)], swap_s.at[ch], mirror_r.at[0, ch], to_straight)

    def pass_copy(ch):
        at = pl.ds(ch * sub, sub)
        slot = (z - x + 4) % 4 - 1
        return copy(
            mirror_out.at[mirror_part(1, ch)], passing.at[slot, at], mirror_s.at[1, ch], pass_r.at[slot, ch], pass_out
        )

    def passing_copy(slot, ch):
        at = pl.ds(ch * sub, sub)
        return copy(
            passing.at[slot, at], mirror_in.at[mirror_part(1, ch)], pass_s.at[slot, ch], mirror_r.at[1, ch], pass_on[slot]
        )

    def arriving(slot, ch):
        at = pl.ds(ch * sub, sub)
        return copy(
            mirror_out.at[mirror_part(1, ch)], passing.at[slot, at], mirror_s.at[1, ch], pass_r.at[slot, ch], pass_from[slot]
        )

    def by_hops(ch):
        return ch < CHUNKS - DIRECT

    def hop_copy(p, ch):
        at = pl.ds(ch * sub, sub)
        return copy(
            mirror_out.at[mirror_part(p, ch)], passing.at[p, at], mirror_s.at[p, ch], pass_r.at[p, ch], hop_out
        )

    def hop_on(p, ch):
        at = pl.ds(ch * sub, sub)
        return copy(
            passing.at[p, at], mirror_in.at[mirror_part(p, ch)], pass_s.at[p, ch], mirror_r.at[p, ch], hop_to
        )

    def layer_copy(ch):
        at = part(lay, ch)
        return copy(same0.at[at], same0.at[at], layer_s.at[ch], layer_r.at[ch], to_layer)

    def y_copy(ch):
        return copy(same0.at[part(1 - lay, ch)], left.at[1, piece(ch)], y_s.at[ch], y_r.at[ch], to_y)

    def x_copy(way, s, ch):
        slot = (6 if way == 0 else 2) + s
        return copy(left.at[s, piece(ch)], left.at[slot, piece(ch)], x_s.at[way, s, ch], x_r.at[way, s, ch], to_x[way])

    aside = (CHUNKS - ASIDE, 0)

    def kept(way, ch, act):
        @pl.when(ch < aside[0] if way == 0 else ch >= ASIDE)
        def _():
            act()

    def pair_copy(way):
        slot = 6 if way == 0 else 2
        at = pl.ds(aside[way] * step, ASIDE * step)
        return copy(left.at[slot, at], left.at[slot + 1, at], pair_s.at[way], pair_r.at[way], to_pair)

    def side_copy(way):
        tile = same3 if way == 0 else same1
        at = pl.ds(lay * half + aside[way] * step, ASIDE * step)
        return copy(tile.at[at], tile.at[at], side_s.at[way], side_r.at[way], to_layer)

    def x_forward(way, s, ch):
        slot = (6 if way == 0 else 2) + s
        return copy(left.at[slot, piece(ch)], left.at[4 + s, piece(ch)], xf_s.at[s, ch], xf_r.at[s, ch], to_x[way])

    def z_copy(way, d, ch):
        at = part(half_of(d), ch)
        target = same3 if way == 0 else same1
        return copy(same0.at[at], target.at[at], z_s.at[way, d, ch], z_r.at[way, d, ch], to_z[way])

    def z_forward(way, d, ch):
        at = part(half_of(d), ch)
        source = same3 if way == 0 else same1
        return copy(source.at[at], same2.at[at], zf_s.at[d, ch], zf_r.at[d, ch], to_z[way])

    def one_way(ch, start):
        @pl.when(ch < CHUNKS // 2)
        def _():
            start(0)

        @pl.when(ch >= CHUNKS // 2)
        def _():
            start(1)

    def core_copy(dz, d, ch):
        at = part(half_of(d), ch)
        return copy(same[dz].at[at], other[dz].at[at], core_s.at[dz, d, ch], core_r.at[dz, d, ch], to_core)

    def each(body):
        def run(ch, carry):
            body(ch)
            return carry

        lax.fori_loop(0, CHUNKS, run, 0)

    greeted = jnp.where(on_ring, 4, 3) + jnp.where(helps, 2, 0)
    greeted += jnp.where(jnp.logical_and(crossed, jnp.logical_not(far_off)), 1, 0)
    pl.semaphore_wait(barrier, 8 + greeted)

    load.wait()

    def send_mirrored(ch):
        def pick(n, carry):
            at = ch * step + n
            source = pattern[col, row, lay * half + at]
            mirror_out[at] = stored[jnp.maximum(source, 0)].T
            return carry

        lax.fori_loop(0, step, pick, 0)

        @pl.when(on_ring)
        def _():
            mirror_copy(0, ch, to_crossed).start()
            mirror_copy(1, ch, to_crossed).start()

        @pl.when(jnp.logical_and(far_off, by_hops(ch)))
        def _():
            hop_copy(0, ch).start()
            hop_copy(1, ch).start()

        @pl.when(jnp.logical_and(far_off, jnp.logical_not(by_hops(ch))))
        def _():
            mirror_copy(0, ch, to_mirror).start()
            mirror_copy(1, ch, to_mirror).start()

        @pl.when(near_by)
        def _():
            @pl.when(crossed)
            def _():
                swap_copy(ch).start()

            @pl.when(jnp.logical_not(crossed))
            def _():
                mirror_copy(0, ch, to_straight).start()

            pass_copy(ch).start()

    @pl.when(off_diagonal)
    def _():
        each(send_mirrored)

    def clear(n, carry):
        out[n] = jnp.zeros(out.shape[1:], out.dtype)
        return carry

    lax.fori_loop(0, half, clear, 0)

    def send_on(ch):
        @pl.when(crossed)
        def _():
            swap_copy(ch).wait_recv()
            swap_on(ch).start()

        @pl.when(jnp.logical_and(helps, by_hops(ch)))
        def _():
            for p in range(2):
                hop_copy(p, ch).wait_recv()
                hop_on(p, ch).start()

    @pl.when(near_by)
    def _():
        each(send_on)

    def pass_along(ch):
        for slot in (0, 2):
            arriving(slot, ch).wait_recv()
            passing_copy(slot, ch).start()

    @pl.when(on_ring)
    def _():
        each(pass_along)

    def complete(ch):
        @pl.when(off_diagonal)
        def _():
            mirror_copy(0, ch, to_straight).wait_recv()
            mirror_copy(1, ch, to_straight).wait_recv()

            def choose(n, carry):
                at = ch * step + n
                r = lay * half + at
                c = jnp.maximum(pattern[row, col, r], 0)
                upper = r * 8 + row <= c * 8 + col
                block = jnp.where(upper, stored[r], mirror_in[at])
                same0[r] = block
                left[0, at] = block
                return carry

            lax.fori_loop(0, step, choose, 0)

        @pl.when(jnp.logical_not(off_diagonal))
        def _():
            def take(n, carry):
                at = ch * step + n
                block = stored[lay * half + at]
                same0[lay * half + at] = block
                left[0, at] = block
                return carry

            lax.fori_loop(0, step, take, 0)

        layer_copy(ch).start()
        for way in range(2):
            x_copy(way, 0, ch).start()
            z_copy(way, 0, ch).start()
        core_copy(0, 0, ch).start()

    each(complete)

    def spread_layer(ch):
        layer_copy(ch).wait_recv()
        y_copy(ch).start()
        for way in range(2):
            kept(way, ch, z_copy(way, 1, ch).start)
        core_copy(0, 1, ch).start()

    each(spread_layer)

    def forward_own(ch):
        for way in range(2):
            x_copy(way, 0, ch).wait_recv()
        one_way(ch, lambda way: x_forward(way, 0, ch).start())
        for way in range(2):
            z_copy(way, 0, ch).wait_recv()
        one_way(ch, lambda way: z_forward(way, 0, ch).start())
        for dz in (1, 3):
            core_copy(dz, 0, ch).start()
        for way in range(2):
            @pl.when(ch == aside[way] + ASIDE - 1)
            def _(way=way):
                side_copy(way).start()
                pair_copy(way).start()

    def spread_y(ch):
        y_copy(ch).wait_recv()
        for way in range(2):
            kept(way, ch, x_copy(way, 1, ch).start)

    each(spread_y)
    each(forward_own)

    def forward_second(ch):
        for way in range(2):
            kept(way, ch, x_copy(way, 1, ch).wait_recv)
        one_way(ch, lambda way: x_forward(way, 1, ch).start())
        for way in range(2):
            kept(way, ch, z_copy(way, 1, ch).wait_recv)
        one_way(ch, lambda way: z_forward(way, 1, ch).start())
        for way, dz in ((0, 3), (1, 1)):
            kept(way, ch, core_copy(dz, 1, ch).start)

    each(forward_second)
    for way, dz in ((0, 3), (1, 1)):
        side_copy(way).wait_recv()
        for n in range(ASIDE):
            core_copy(dz, 1, aside[way] + n).start()
        pair_copy(way).wait_recv()

    def near(ch):
        for dz in (0, 1, 3):
            for d in range(2):
                core_copy(dz, d, ch).wait_recv()

    each(near)

    def multiply(dz, differs):
        tile = (other if differs else same)[dz]
        m = 2 * ((z + dz) % 4) + (k + differs) % 2
        slot = 2 * ((m // 2 + 4 - x) % 4) + (m % 2 + yh) % 2

        def one(n, carry):
            r = lay * half + n
            c = pattern[row, m, r]
            inner = jnp.maximum(c, 0)
            t = pattern[m, col, inner]
            present = jnp.logical_and(c >= 0, t >= 0)
            block = product(left[slot, n], tile[inner])
            for q in range(2):
                matched = jnp.logical_and(present, wanted[q, r] == t)
                out[n, q] += block * jnp.where(matched, 1.0, 0.0)
            return carry

        lax.fori_loop(0, half, one, 0, unroll=8)

    def far(dz):
        return (z + dz - x + 4) % 4 == 2

    for dz in (0, 1, 3):
        @pl.when(jnp.logical_not(far(dz)))
        def _(dz=dz):
            multiply(dz, 0)
            multiply(dz, 1)

    def last(ch):
        for d in range(2):
            z_forward(0, d, ch).wait_recv()
            core_copy(2, d, ch).start()
            x_forward(0, d, ch).wait_recv()

    each(last)

    for dz in (0, 1, 3):
        @pl.when(far(dz))
        def _(dz=dz):
            multiply(dz, 0)
            multiply(dz, 1)

    multiply(2, 0)

    def last_core(ch):
        for d in range(2):
            core_copy(2, d, ch).wait_recv()

    each(last_core)
    multiply(2, 1)

    def drain(ch):
        @pl.when(off_diagonal)
        def _():
            mirror_copy(0, ch, to_straight).wait_send()
            mirror_copy(1, ch, to_straight).wait_send()

        @pl.when(jnp.logical_and(crossed, near_by))
        def _():
            swap_on(ch).wait_send()

        @pl.when(on_ring)
        def _():
            for slot in (0, 2):
                passing_copy(slot, ch).wait_send()

        @pl.when(jnp.logical_and(helps, by_hops(ch)))
        def _():
            for p in range(2):
                hop_on(p, ch).wait_send()

        layer_copy(ch).wait_send()
        y_copy(ch).wait_send()
        for way in range(2):
            x_forward(0, way, ch).wait_send()
            z_forward(0, way, ch).wait_send()
            x_copy(way, 0, ch).wait_send()
            z_copy(way, 0, ch).wait_send()
            kept(way, ch, x_copy(way, 1, ch).wait_send)
            kept(way, ch, z_copy(way, 1, ch).wait_send)
        for dz in range(4):
            for d in range(2):
                core_copy(dz, d, ch).wait_send()

    each(drain)
    for way in range(2):
        side_copy(way).wait_send()
        pair_copy(way).wait_send()


def per_device(stored_blocks, pattern, result_cols):
    tile = stored_blocks[0, 0]
    rows, size = tile.shape[0], tile.shape[-1]
    half = rows // 2
    vmem = pl.BlockSpec(memory_space=pltpu.VMEM)
    smem = pl.BlockSpec(memory_space=pltpu.SMEM)
    sems = pltpu.SemaphoreType.DMA
    block = (size, size)
    result = pl.pallas_call(
        functools.partial(kernel, rows),
        out_shape=jax.ShapeDtypeStruct((half, 2, *block), jnp.float32),
        in_specs=[smem, smem, pl.BlockSpec(memory_space=pl.ANY)],
        out_specs=vmem,
        scratch_shapes=[
            pltpu.VMEM((rows, *block), jnp.float32),
            sems(()),
            pltpu.VMEM((half, *block), jnp.float32),
            pltpu.VMEM((half, *block), jnp.float32),
            pltpu.VMEM((half // 2, *block), jnp.float32),
            pltpu.VMEM((3, half // 2, *block), jnp.float32),
            pltpu.VMEM((8, half, *block), jnp.float32),
            *[pltpu.VMEM((rows, *block), jnp.float32)] * 8,
            *[sems((2, CHUNKS))] * 2,
            *[sems((CHUNKS,))] * 2,
            *[sems((3, CHUNKS))] * 2,
            *[sems((CHUNKS,))] * 4,
            *[sems((2, 2, CHUNKS))] * 2,
            *[sems((2,))] * 4,
            *[sems((2, CHUNKS))] * 2,
            *[sems((2, 2, CHUNKS))] * 2,
            *[sems((2, CHUNKS))] * 2,
            *[sems((4, 2, CHUNKS))] * 2,
        ],
        compiler_params=pltpu.CompilerParams(
            collective_id=0, has_side_effects=True, vmem_limit_bytes=58 * 2**20
        ),
    )(pattern, result_cols[0, 0].T, tile)
    return result[None, None]


def solution(mesh):
    return jax.shard_map(
        per_device,
        mesh=mesh,
        in_specs=(P("row", "col", None, None, None), P(), P("row", "col", None, None)),
        out_specs=P("row", "col", "layer", None, None, None),
        check_vma=False,
    )
```
